128 devices in a mesh: group: 2 (over y_hi), tile: 64 (over x, y_lo, z, core).
Axes of the slice: x: 4, y: 4 (y_hi: 2, y_lo: 2; y = y_hi * 2 + y_lo), z: 4, core: 2. Of those that a mesh axis runs over, the one named last changes fastest.
Arguments:
- pressure: float32 [60, 1536, 384], P(None, ('group', 'tile')), may hold values from -6 to 6
- wind_x: float32 [60, 1536, 384], P(None, ('group', 'tile')), may hold values from -6 to 6
- wind_y: float32 [60, 1536, 384], P(None, ('group', 'tile')), may hold values from -6 to 6
- courant: float32 [60], replicated, may hold values from 0.2 to 0.6
- send_list: int32 [128, 128, 36], P(('group', 'tile')), may hold values from -1 to 4607, as said below
- norm_gain: float32 [180], replicated, may hold values from 0.25 to 1.75
- w_first: bfloat16 [180, 1024], replicated, may hold values from -0.4375 to 0.4375
- b_first: float32 [1024], replicated, may hold values from -3 to 3
- w_second: bfloat16 [1024, 1024], replicated, may hold values from -0.1875 to 0.1875
- b_second: float32 [1024], replicated, may hold values from -3 to 3
- w_last: bfloat16 [1024, 180], replicated, may hold values from -0.1875 to 0.1875
Outputs:
- new_pressure: float32 [60, 1536, 384], P(None, ('group', 'tile'))
- new_wind_x: float32 [60, 1536, 384], P(None, ('group', 'tile'))
- new_wind_y: float32 [60, 1536, 384], P(None, ('group', 'tile'))
The draws below stay inside these ranges and needn't reach their ends.
Inputs may be any that keep to these rules, and one draw needn't show every extreme that they name: For each device d there is a count v_d: in every send_list[d, j] the first v_d entries are local columns of d and the rest are -1; no column is listed twice. In each aligned four of devices one has v_d = 36 and the four counts add up to 48, so each physics shard treats 1536 columns.
All inputs are finite; a program needn't handle non-finite values.
Results may differ from the reference program's by a relative error of at most 0.0015.
Values may be sent and summed in bfloat16 or wider, within the bound.
No kernel may reach another device: no remote copies, remote signals or barrier semaphores. Data moves between devices by JAX's collectives and lax.ppermute only.
A program may use at most 128 MiB of HBM per device.

```python
import math
import jax
import jax.numpy as jnp
from jax import lax

LEVELS = 60
UNITS = 1024
NY = 384
SUBSTEPS = 6
NX = 1536
COLS_DEV = 4608
SLOTS = 36
ROWS_PHYS = 1536
N_GROUP = 2
N_TILE = 64


def draw_send_list(key, part):
    key = jax.random.fold_in(key, 7)
    devices = N_GROUP * N_TILE
    key_cut, key_where, key_perm = jax.random.split(key, 3)
    groups = devices // 4
    extra = SLOTS // 3
    cuts = jax.random.randint(key_cut, (groups, 2), 0, extra + 1)
    lower = jnp.min(cuts, axis=1)
    upper = jnp.max(cuts, axis=1)
    base = jnp.stack([jnp.full((groups,), SLOTS, jnp.int32), lower, upper - lower, extra - upper], axis=1).astype(jnp.int32)
    where_full = jax.random.randint(key_where, (groups,), 0, 4)
    turned = (jnp.arange(4)[None, :] - where_full[:, None]) % 4
    counts = jnp.take_along_axis(base, turned, axis=1).reshape(devices)
    orders = jax.vmap(lambda single: jax.random.permutation(single, COLS_DEV))(jax.random.split(key_perm, devices))
    slot_index = jnp.arange(SLOTS)
    target = jnp.arange(devices)
    position = target[None, :, None] * counts[:, None, None] + slot_index[None, None, :]
    position = jnp.minimum(position, COLS_DEV - 1).reshape(devices, devices * SLOTS)
    picked = jnp.take_along_axis(orders, position, axis=1).reshape(devices, devices, SLOTS)
    return jnp.where(slot_index[None, None, :] < counts[:, None, None], picked, -1).astype(jnp.int32)


def shard_levels(own_key, shape, pieces, smallest, high):
    gain = 1.0
    for dim, parts in pieces:
        heights = jax.random.uniform(jax.random.fold_in(jax.random.fold_in(own_key, 6), dim), (parts,), jnp.float32, smallest / len(pieces), high / len(pieces))
        gain = gain * jnp.repeat(jnp.exp(heights), shape[dim] // parts).reshape((-1,) + (1,) * (len(shape) - 1 - dim))
    return gain


def scatter_about(own_key, dims, scale, most, shards=(), kind=jnp.bfloat16):
    loudness = shard_levels(own_key, dims, shards, -0.22, 0.18) if shards else 1.0
    values = jax.random.normal(own_key, dims, jnp.float32) * scale * loudness
    return jnp.minimum(jnp.maximum(values, -most), most).astype(kind)


def setup_inputs(seed: int = 0) -> dict:
    keys = jax.random.split(jax.random.key(seed), 12)
    pressure = scatter_about(keys[0], (LEVELS, NX, NY), 1.0, 6.0, ((1, 128),), jnp.float32)
    wind_x = scatter_about(keys[1], (LEVELS, NX, NY), 1.0, 6.0, ((1, 128),), jnp.float32)
    wind_y = scatter_about(keys[2], (LEVELS, NX, NY), 1.0, 6.0, ((1, 128),), jnp.float32)
    courant = jnp.clip(jnp.exp(jax.random.uniform(keys[3], (LEVELS,), jnp.float32, math.log(0.2), math.log(0.6))), 0.2, 0.6)
    send_list = draw_send_list(jax.random.fold_in(keys[11], 71), 0)
    norm_gain = jnp.clip(1.0 + 0.15 * jax.random.normal(keys[5], (3 * LEVELS,), jnp.float32), 0.25, 1.75)
    w_first = scatter_about(keys[6], (3 * LEVELS, UNITS), (3 * LEVELS) ** -0.5, 0.4375)
    b_first = scatter_about(keys[7], (UNITS,), 0.5, 3.0, (), jnp.float32)
    w_second = scatter_about(keys[8], (UNITS, UNITS), UNITS ** -0.5, 0.1875)
    b_second = scatter_about(keys[9], (UNITS,), 0.5, 3.0, (), jnp.float32)
    w_last = scatter_about(keys[10], (UNITS, 3 * LEVELS), UNITS ** -0.5, 0.1875)
    return dict(pressure=pressure, wind_x=wind_x, wind_y=wind_y, courant=courant, send_list=send_list, norm_gain=norm_gain, w_first=w_first, b_first=b_first, w_second=w_second, b_second=b_second, w_last=w_last)


def acoustic(fields, factor, walled, eastern, western):
    pressure, along_x, along_y = fields
    right_side = jnp.concatenate([pressure[:, 1:], eastern(pressure)], axis=1)
    along_x = along_x - factor * (right_side - pressure)
    north_diff = jnp.concatenate([pressure[:, :, 1:] - pressure[:, :, :-1], jnp.zeros_like(pressure[:, :, :1])], axis=2)
    along_y = (along_y - factor * north_diff) * walled
    left_side = jnp.concatenate([western(along_x), along_x[:, :-1]], axis=1)
    south_side = jnp.concatenate([jnp.zeros_like(along_y[:, :, :1]), along_y[:, :, :-1]], axis=2)
    pressure = pressure - factor * (along_x - left_side) - factor * (along_y - south_side)
    return (pressure, along_x, along_y)

def column_mlp(columns, norm_gain, w_first, b_first, w_second, b_second, w_last):
    values = columns.astype(jnp.float32)
    scaled = values * lax.rsqrt(lax.optimization_barrier(jnp.mean(values * values, axis=0, keepdims=True)) + 1e-05) * norm_gain[:, None]
    normed = scaled.astype(jnp.bfloat16)
    inner = (((0,), (0,)), ((), ()))
    hidden_one = jax.nn.silu(lax.dot_general(w_first, normed, inner, preferred_element_type=jnp.float32) + b_first[:, None]).astype(jnp.bfloat16)
    hidden_two = jax.nn.silu(lax.dot_general(w_second, hidden_one, inner, preferred_element_type=jnp.float32) + b_second[:, None]).astype(jnp.bfloat16)
    return lax.dot_general(w_last, hidden_two, inner, preferred_element_type=jnp.float32).astype(jnp.bfloat16)

def wrap_east(field):
    return field[:, :1]

def wrap_west(field):
    return field[:, -1:]

def reference(pressure, wind_x, wind_y, courant, send_list, norm_gain, w_first, b_first, w_second, b_second, w_last):
    factor = courant[:, None, None]
    walled = (jnp.arange(NY) < NY - 1).astype(jnp.float32)[None, None, :]
    fields = (pressure, wind_x, wind_y)
    middle = fields
    for substep in range(SUBSTEPS):
        fields = acoustic(fields, factor, walled, wrap_east, wrap_west)
        if substep == SUBSTEPS // 2 - 1:
            middle = fields
    features = jnp.concatenate(middle, axis=0).reshape(3 * LEVELS, NX * NY).astype(jnp.bfloat16)
    devices = N_GROUP * N_TILE
    global_ids = (jnp.arange(devices, dtype=jnp.int32)[:, None, None] * COLS_DEV + send_list).reshape(-1).astype(jnp.int32)
    valid = send_list.reshape(-1) >= 0
    picked = jnp.nonzero(valid, size=devices * ROWS_PHYS)[0].astype(jnp.int32)
    chosen = global_ids[picked].reshape(devices, ROWS_PHYS)

    def one_block(ids):
        return column_mlp(jnp.take(features, ids, axis=1), norm_gain, w_first, b_first, w_second, b_second, w_last)
    outputs = lax.map(one_block, chosen)
    moved = jnp.moveaxis(outputs, 1, 0).reshape(3 * LEVELS, devices * ROWS_PHYS).astype(jnp.float32)
    tendency = jnp.zeros((3 * LEVELS, NX * NY), jnp.float32).at[:, chosen.reshape(-1)].add(moved)
    tendency = tendency.reshape(3, LEVELS, NX, NY)
    return (fields[0] + tendency[0], fields[1] + tendency[1], fields[2] + tendency[2])
```

```python
import jax
import jax.numpy as jnp
from jax import lax
from jax.experimental import pallas as pl
from jax.experimental.pallas import tpu as pltpu
from jax.sharding import PartitionSpec as P

AXES = ("group", "tile")
LEVELS, WIDTH, ACROSS, UNITS, SLOTS, DEVICES = 60, 12, 384, 1024, 36, 128
ROWS = 3 * LEVELS
HALO = 6
SPAN = WIDTH + 2 * HALO
CHUNK = 2 * ACROSS
TILE = 256
F32, BF16 = jnp.float32, jnp.bfloat16
NN = (((1,), (0,)), ((), ()))
NT = (((1,), (1,)), ((), ()))
ANY = pl.BlockSpec(memory_space=pl.ANY)
VMEM = pl.BlockSpec(memory_space=pltpu.VMEM)


def lanes(shape):
    return lax.broadcasted_iota(jnp.int32, shape, len(shape) - 1)


def run_copies(pairs, sems, first=0):
    copies = [
        pltpu.make_async_copy(src, dst, sems.at[first + i]) for i, (src, dst) in enumerate(pairs)
    ]
    for copy in copies:
        copy.start()
    return copies


def edges_kernel(p_hbm, u_hbm, v_hbm, to_next, to_prev, u_mem, v_mem, r_mem, l_mem, sems):
    loads = run_copies([(u_hbm, u_mem), (v_hbm, v_mem)], sems)
    plain = run_copies(
        [
            (p_hbm.at[WIDTH - HALO :], to_next.at[:HALO]),
            (p_hbm.at[:HALO], to_prev.at[:HALO]),
        ],
        sems,
        2,
    )
    for copy in loads:
        copy.wait()

    def divergence(x):
        v = v_mem[x]
        v = jnp.where(lanes(v.shape) < ACROSS - 1, v, 0.0)
        return v - pltpu.roll(v, 1, 1)

    total = jnp.zeros((LEVELS, ACROSS), F32)
    for i in range(HALO):
        x = WIDTH - 1 - i
        r_mem[HALO - 1 - i] = u_mem[x] - total
        if i < HALO - 1:
            total = total + divergence(x)
    total = jnp.zeros((LEVELS, ACROSS), F32)
    for x in range(HALO):
        total = total + divergence(x)
        l_mem[x] = u_mem[x] + total
    stores = run_copies(
        [(r_mem, to_next.at[HALO:]), (l_mem, to_prev.at[HALO:])],
        sems,
        4,
    )
    for copy in plain + stores:
        copy.wait()


def edges(p, u, v):
    shape = jax.ShapeDtypeStruct((2 * HALO, LEVELS, ACROSS), F32)
    return pl.pallas_call(
        edges_kernel,
        out_shape=(shape, shape),
        in_specs=[ANY] * 3,
        out_specs=(ANY, ANY),
        scratch_shapes=[
            pltpu.VMEM((WIDTH, LEVELS, ACROSS), F32),
            pltpu.VMEM((WIDTH, LEVELS, ACROSS), F32),
            pltpu.VMEM((HALO, LEVELS, ACROSS), F32),
            pltpu.VMEM((HALO, LEVELS, ACROSS), F32),
            pltpu.SemaphoreType.DMA((6,)),
        ],
        name="edges",
    )(p, u, v)


def march(count, low, high, square, load_p, load_u, load_v, done):
    ps = [{} for _ in range(count + 1)]
    us = [{} for _ in range(count + 1)]
    vs = [{} for _ in range(count + 1)]

    def advance(k, x):
        here, east = ps[k - 1][x], ps[k - 1][x + 1]
        us[k][x] = us[k - 1][x] - (east - here)
        if x < low + k:
            if k == count:
                done(x, None, us[k][x], None)
            return
        north = pltpu.roll(here, ACROSS - 1, 1)
        v = vs[k - 1][x]
        v = here - north if v is None else v - (north - here)
        v = jnp.where(lanes(v.shape) < ACROSS - 1, v, 0.0)
        vs[k][x] = v
        flow = (us[k][x] - us[k][x - 1]) + (v - pltpu.roll(v, 1, 1))
        ps[k][x] = here - square * flow
        if k == count:
            done(x, ps[k][x], us[k][x], v)
        elif x - 1 >= low + k:
            advance(k + 1, x - 1)

    ps[0][low] = load_p(low)
    for x in range(low, high):
        ps[0][x + 1] = load_p(x + 1)
        us[0][x] = load_u(x)
        if x > low:
            vs[0][x] = load_v(x)
        advance(1, x)


def by_level(row):
    return jnp.broadcast_to(row, (128, row.shape[1])).T


def by_groups(work):
    def group(g, carry):
        work(pl.ds(pl.multiple_of(g * 8, 8), 8))
        return carry

    lax.fori_loop(0, LEVELS // 8, group, 0)
    work(slice(LEVELS // 8 * 8, LEVELS))


def level_constants(courant_row, c_mem):
    c = by_level(courant_row)
    c_mem[0] = c
    c_mem[1] = c * c
    c_mem[2] = 1.0 / c


def group_constants(c_mem, rows):
    wide = lambda i: jnp.concatenate([c_mem[i, rows, :]] * 3, axis=1)
    return wide(0), wide(1), wide(2)


def silu(z):
    half = z * 0.5
    return half + half * jnp.tanh(half)


def normed_columns(state, gain, xs):
    columns = jnp.concatenate(
        [jnp.concatenate([f[x] for f in state], axis=0) for x in xs], axis=1
    )
    values = columns.astype(BF16).astype(F32)
    mean = jnp.sum(values * values, axis=0, keepdims=True) * (1.0 / ROWS)
    return (values * lax.rsqrt(mean + 1e-05) * gain).astype(BF16)


def network(normed, w1, b1, w2, b2, w3, h1, h2):
    rows = normed.T
    for n in range(0, UNITS, TILE):
        z = lax.dot_general(rows, w1[:, n : n + TILE], NN, preferred_element_type=F32)
        h1[:, n : n + TILE] = silu(z + b1[:, n : n + TILE]).astype(BF16)
    for n in range(0, UNITS, TILE):
        z = lax.dot_general(h1[...], w2[:, n : n + TILE], NN, preferred_element_type=F32)
        h2[:, n : n + TILE] = silu(z + b2[:, n : n + TILE]).astype(BF16)
    t = lax.dot_general(h2[...], w3[...], NN, preferred_element_type=F32)
    return t.T.astype(BF16).astype(F32)


def keep_listed(t, mask, x):
    row = jnp.concatenate([mask[3 * x + j : 3 * x + j + 1, :] for j in range(3)], axis=1)
    return jnp.where(row > 0.5, t, 0.0)


def store_tendency(t, mask, xs, places, out):
    for i, (x, place) in enumerate(zip(xs, places)):
        listed = keep_listed(t[:, i * ACROSS : (i + 1) * ACROSS], mask, x)
        for f in range(3):
            out[place, f] = listed[f * LEVELS : (f + 1) * LEVELS]


WEIGHTS_SCRATCH = [
    pltpu.VMEM((ROWS, UNITS), BF16),
    pltpu.VMEM((1, UNITS), F32),
    pltpu.VMEM((UNITS, UNITS), BF16),
    pltpu.VMEM((1, UNITS), F32),
    pltpu.VMEM((ROWS, UNITS), BF16),
    pltpu.VMEM((UNITS, ROWS), BF16),
    pltpu.VMEM((CHUNK, UNITS), BF16),
    pltpu.VMEM((CHUNK, UNITS), BF16),
]


def network_flops(columns):
    return 2 * columns * (2 * ROWS * UNITS + UNITS * UNITS)


def interior_kernel(
    p_hbm, u_hbm, v_hbm, w1_hbm, b1_hbm, w2_hbm, b2_hbm, w3_hbm, courant, gain, lists,
    tend, mask,
    p_mem, u_mem, v_mem, a_mem, b_mem, d_mem, c_mem, one_x, one_y,
    w1, b1, w2, b2, w3t, w3, h1, h2, sems,
):
    fields = run_copies([(p_hbm, p_mem), (u_hbm, u_mem),
                         (v_hbm, v_mem)], sems)
    weights = run_copies([(w1_hbm, w1), (b1_hbm, b1), (w2_hbm, w2), (b2_hbm, b2),
                          (w3_hbm, w3t)], sems, 3)
    level_constants(courant[...], c_mem)
    gain_column = by_level(gain[...])[:, :1]
    for s in range(SLOTS):
        entry = lists[s]
        part, spot = entry >> 7, entry & 127
        where = slice(s * DEVICES, (s + 1) * DEVICES)
        one_x[:, where] = (
            lax.broadcasted_iota(jnp.int32, (48, DEVICES), 0) == part
        ).astype(F32).astype(BF16)
        one_y[:, where] = (
            lax.broadcasted_iota(jnp.int32, (128, DEVICES), 0) == spot
        ).astype(F32).astype(BF16)
    mask[...] = lax.dot_general(one_x[...], one_y[...], NT, preferred_element_type=F32)
    for copy in fields:
        copy.wait()

    def group(rows):
        c, square, inverse = group_constants(c_mem, rows)

        def done(x, p, u, v):
            if p is not None:
                a_mem[x - 3, rows, :] = p
                b_mem[x - 3, rows, :] = u * c
                d_mem[x - 3, rows, :] = v * c

        march(3, 0, WIDTH - 1, square,
              lambda x: p_mem[x, rows, :],
              lambda x: u_mem[x, rows, :] * inverse,
              lambda x: v_mem[x, rows, :] * inverse, done)

    by_groups(group)
    for copy in weights:
        copy.wait()
    w3[...] = w3t[...].T
    for i in range(3):
        xs = (2 * i, 2 * i + 1)
        t = network(normed_columns((a_mem, b_mem, d_mem), gain_column, xs), w1, b1, w2, b2, w3, h1, h2)
        store_tendency(t, mask, [x + 3 for x in xs], xs, tend)


def interior(p, u, v, weights, courant, gain, lists):
    column = pltpu.VMEM((WIDTH, LEVELS, ACROSS), F32)
    middle = pltpu.VMEM((WIDTH // 2, LEVELS, ACROSS), F32)
    return pl.pallas_call(
        interior_kernel,
        out_shape=(
            jax.ShapeDtypeStruct((WIDTH // 2, 3, LEVELS, ACROSS), F32),
            jax.ShapeDtypeStruct((48, 128), F32),
        ),
        in_specs=[ANY] * 8 + [VMEM] * 3,
        out_specs=(VMEM, VMEM),
        scratch_shapes=[column] * 3 + [middle] * 3
        + [pltpu.VMEM((3, LEVELS, 128), F32)]
        + [pltpu.VMEM((48, SLOTS * DEVICES), BF16), pltpu.VMEM((128, SLOTS * DEVICES), BF16)]
        + WEIGHTS_SCRATCH
        + [pltpu.SemaphoreType.DMA((8,))],
        compiler_params=pltpu.CompilerParams(vmem_limit_bytes=44 * 2**20),
        cost_estimate=pl.CostEstimate(
            flops=network_flops(WIDTH // 2 * ACROSS), bytes_accessed=8 * 2**20, transcendentals=0
        ),
        name="interior",
    )(p, u, v, *weights, courant, gain, lists)


def finish_kernel(
    p_hbm, u_hbm, v_hbm, left, right, tend, w1_hbm, b1_hbm, w2_hbm, b2_hbm, w3_hbm,
    mask, courant, gain,
    p_out, u_out, v_out,
    p_mem, u_mem, v_mem, a_mem, b_mem, d_mem, t_mem, c_mem,
    w1, b1, w2, b2, w3t, w3, h1, h2, sems,
):
    own = slice(HALO, HALO + WIDTH)
    fields = run_copies(
        [
            (p_hbm, p_mem.at[own]),
            (u_hbm, u_mem.at[own]),
            (v_hbm, v_mem.at[own]),
            (left.at[:HALO], p_mem.at[:HALO]),
            (left.at[HALO:], u_mem.at[:HALO]),
            (right.at[:HALO], p_mem.at[HALO + WIDTH :]),
            (right.at[HALO:], u_mem.at[HALO + WIDTH :]),
        ],
        sems,
    )
    weights = run_copies([(w1_hbm, w1), (b1_hbm, b1), (w2_hbm, w2), (b2_hbm, b2),
                          (w3_hbm, w3t), (tend, t_mem.at[3:9])], sems, 7)
    level_constants(courant[...], c_mem)
    gain_column = by_level(gain[...])[:, :1]
    for copy in fields:
        copy.wait()

    def first_half(rows):
        c, square, inverse = group_constants(c_mem, rows)

        def done(x, p, u, v):
            u_mem[x + HALO, rows, :] = u
            if p is None:
                return
            p_mem[x + HALO, rows, :] = p
            v_mem[x + HALO, rows, :] = v
            if 0 <= x < 3 or 9 <= x < 12:
                at = x if x < 3 else x - 6
                a_mem[at, rows, :] = p
                b_mem[at, rows, :] = u * c
                d_mem[at, rows, :] = v * c

        march(3, -HALO, WIDTH + HALO - 1, square,
              lambda x: p_mem[x + HALO, rows, :],
              lambda x: u_mem[x + HALO, rows, :] * inverse,
              lambda x: v_mem[x + HALO, rows, :] * inverse if 0 <= x < WIDTH else None, done)

    by_groups(first_half)
    for copy in weights:
        copy.wait()
    w3[...] = w3t[...].T
    columns = (0, 1, 2, 9, 10, 11)
    for i in range(3):
        places = (2 * i, 2 * i + 1)
        xs = [columns[j] for j in places]
        t = network(normed_columns((a_mem, b_mem, d_mem), gain_column, places), w1, b1, w2, b2, w3, h1, h2)
        store_tendency(t, mask, xs, xs, t_mem)

    def second_half(rows):
        c, square, inverse = group_constants(c_mem, rows)

        def done(x, p, u, v):
            if p is None:
                return
            p_mem[x, rows, :] = p + t_mem[x, 0, rows, :]
            u_mem[x, rows, :] = u * c + t_mem[x, 1, rows, :]
            v_mem[x, rows, :] = v * c + t_mem[x, 2, rows, :]

        march(3, -3, WIDTH + 2, square,
              lambda x: p_mem[x + HALO, rows, :],
              lambda x: u_mem[x + HALO, rows, :],
              lambda x: v_mem[x + HALO, rows, :], done)

    by_groups(second_half)
    outs = run_copies(
        [(m.at[:WIDTH], o) for m, o in ((p_mem, p_out), (u_mem, u_out), (v_mem, v_out))],
        sems,
    )
    for copy in outs:
        copy.wait()


def finish(p, u, v, left, right, tend, weights, mask, courant, gain):
    shape = jax.ShapeDtypeStruct((WIDTH, LEVELS, ACROSS), F32)
    span = pltpu.VMEM((SPAN, LEVELS, ACROSS), F32)
    half = pltpu.VMEM((WIDTH // 2, LEVELS, ACROSS), F32)
    return pl.pallas_call(
        finish_kernel,
        out_shape=(shape,) * 3,
        in_specs=[ANY] * 11 + [VMEM] * 3,
        out_specs=(ANY,) * 3,
        scratch_shapes=[span] * 3 + [half] * 3
        + [pltpu.VMEM((WIDTH, 3, LEVELS, ACROSS), F32), pltpu.VMEM((3, LEVELS, 128), F32)]
        + WEIGHTS_SCRATCH
        + [pltpu.SemaphoreType.DMA((13,))],
        compiler_params=pltpu.CompilerParams(vmem_limit_bytes=50 * 2**20),
        cost_estimate=pl.CostEstimate(
            flops=network_flops(WIDTH // 2 * ACROSS), bytes_accessed=12 * 2**20, transcendentals=0
        ),
        name="finish",
    )(p, u, v, left, right, tend, *weights, mask, courant, gain)


def body(
    pressure, wind_x, wind_y, courant, send_list,
    norm_gain, w_first, b_first, w_second, b_second, w_last,
):
    p, u, v = [jnp.transpose(f, (1, 0, 2)) for f in (pressure, wind_x, wind_y)]
    courant, gain = courant.reshape(1, LEVELS), norm_gain.reshape(1, ROWS)
    lists = jnp.transpose(send_list, (2, 0, 1))
    weights = (w_first, b_first.reshape(1, UNITS), w_second, b_second.reshape(1, UNITS), w_last.T)
    to_next, to_prev = edges(p, u, v)
    left = lax.ppermute(to_next, AXES, [(i, (i + 1) % DEVICES) for i in range(DEVICES)])
    right = lax.ppermute(to_prev, AXES, [(i, (i - 1) % DEVICES) for i in range(DEVICES)])
    tend, mask = interior(p, u, v, weights, courant, gain, lists)
    outs = finish(p, u, v, left, right, tend, weights, mask, courant, gain)
    return tuple(jnp.transpose(f, (1, 0, 2)) for f in outs)


def solution(mesh):
    split = P(None, AXES, None)
    in_specs = (split,) * 3 + (P(), P(AXES, None, None)) + (P(),) * 6
    return jax.shard_map(
        body, mesh=mesh, in_specs=in_specs, out_specs=(split,) * 3, check_vma=False
    )
```

```python
import jax
import jax.numpy as jnp
from jax import lax
from jax.experimental import pallas as pl
from jax.experimental.pallas import tpu as pltpu
from jax.sharding import PartitionSpec as P

AXES = ("group", "tile")
LEVELS, WIDTH, ACROSS, UNITS, SLOTS, DEVICES = 60, 12, 384, 1024, 36, 128
ROWS = 3 * LEVELS
HALO = 6
SPAN = WIDTH + 2 * HALO
CHUNK = 2 * ACROSS
TILE = 256
F32, BF16 = jnp.float32, jnp.bfloat16
NN = (((1,), (0,)), ((), ()))
NT = (((1,), (1,)), ((), ()))
ANY = pl.BlockSpec(memory_space=pltpu.HBM)
VMEM = pl.BlockSpec(memory_space=pltpu.VMEM)


def lanes(shape):
    return lax.broadcasted_iota(jnp.int32, shape, len(shape) - 1)


def split(value):
    return [value[:, i : i + 128] for i in range(0, ACROSS, 128)]


def join(parts):
    return jnp.concatenate(parts, axis=1)


def run_copies(pairs, sems, first=0):
    copies = [
        pltpu.make_async_copy(src, dst, sems.at[first + i]) for i, (src, dst) in enumerate(pairs)
    ]
    for copy in copies:
        copy.start()
    return copies


def divergence(v):
    v = jnp.where(lanes(v.shape) < ACROSS - 1, v, 0.0)
    return v - pltpu.roll(v, 1, 1)


def edges_kernel(p_hbm, u_hbm, v_hbm, to_next, to_prev, p_mem, u_mem, v_mem, r_mem, l_mem, sems):
    low, high = slice(0, HALO), slice(WIDTH - HALO, WIDTH)
    loads = run_copies(
        [(f.at[s], m.at[s]) for s in (high, low)
         for f, m in ((p_hbm, p_mem), (u_hbm, u_mem), (v_hbm, v_mem))],
        sems,
    )
    for copy in loads[:3]:
        copy.wait()
    for i in range(HALO):
        r_mem[i] = p_mem[WIDTH - HALO + i].astype(BF16)
    for i in range(HALO - 1):
        x = WIDTH - HALO + 1 + i
        r_mem[HALO + i] = ((u_mem[x] - u_mem[x - 1]) + divergence(v_mem[x])).astype(BF16)
    r_mem[2 * HALO - 1] = u_mem[WIDTH - 1].astype(BF16)
    out_next = run_copies([(r_mem, to_next)], sems, 6)
    for copy in loads[3:]:
        copy.wait()
    for i in range(HALO):
        l_mem[i] = p_mem[i].astype(BF16)
    for x in range(HALO):
        west = u_mem[x - 1] if x else 0.0
        l_mem[HALO + x] = ((u_mem[x] - west) + divergence(v_mem[x])).astype(BF16)
    for copy in out_next + run_copies([(l_mem, to_prev)], sems, 7):
        copy.wait()


def edges(p, u, v):
    shape = jax.ShapeDtypeStruct((2 * HALO, LEVELS, ACROSS), BF16)
    return pl.pallas_call(
        edges_kernel,
        out_shape=(shape, shape),
        in_specs=[ANY] * 3,
        out_specs=(ANY, ANY),
        scratch_shapes=[pltpu.VMEM((WIDTH, LEVELS, ACROSS), F32)] * 3
        + [pltpu.VMEM((2 * HALO, LEVELS, ACROSS), BF16)] * 2
        + [pltpu.SemaphoreType.DMA((8,))],
        compiler_params=pltpu.CompilerParams(vmem_limit_bytes=60 * 2**20),
        name="edges",
    )(p, u, v)


def march(count, low, high, square, load_p, load_d, done):
    ps = [{} for _ in range(count + 1)]
    ds = [{} for _ in range(count + 1)]
    sums = {}
    lane = lanes(square.shape)
    first, last = lane == 0, lane == 127

    def substep(k, x):
        west, here, east = (ps[k - 1][x + i] for i in (-1, 0, 1))
        down = [pltpu.roll(h, 127, 1) for h in here]
        up = [pltpu.roll(h, 1, 1) for h in here]
        north = [jnp.where(last, down[1], down[0]), jnp.where(last, down[2], down[1]),
                 jnp.where(last, here[2], down[2])]
        south = [jnp.where(first, here[0], up[0]), jnp.where(first, up[0], up[1]),
                 jnp.where(first, up[1], up[2])]
        ds[k][x] = [d - (((e + w) + (n + s)) - 4.0 * h)
                    for d, e, w, n, s, h in zip(ds[k - 1][x], east, west, north, south, here)]
        ps[k][x] = [h - square * d for h, d in zip(here, ds[k][x])]
        if k == count:
            done(x, ps[k][x], sums[x], sums[x + 1])
        elif low + count - 1 <= x <= high - count + 1:
            sums[x] = [s + p for s, p in zip(sums[x], ps[k][x])]

    for t in range(low, high + 2 * count + 1):
        if t <= high:
            ps[0][t] = load_p(t)
            if low + count - 1 <= t <= high - count + 1:
                sums[t] = ps[0][t]
            if low < t < high:
                ds[0][t] = load_d(t)
        for k in range(1, count + 1):
            x = t - 2 * k
            if low + k <= x <= high - k:
                substep(k, x)


def own_divergence(u, west, v, inverse):
    lane = lanes(inverse.shape)
    first, last = lane == 0, lane == 127
    v = [v[0], v[1], jnp.where(last, 0.0, v[2])]
    up = [pltpu.roll(a, 1, 1) for a in v]
    south = [jnp.where(first, up[i - 1], up[i]) for i in range(3)]
    return [((a - w) + (b - s)) * inverse for a, w, b, s in zip(u, west, v, south)]


def winds(u, v, c, here, east):
    last = lanes(c.shape) == 127
    down = [pltpu.roll(s, 127, 1) for s in here]
    north = [jnp.where(last, down[1], down[0]), jnp.where(last, down[2], down[1]), down[2]]
    u = [a - c * (e - s) for a, e, s in zip(u, east, here)]
    v = [a - c * (n - s) for a, n, s in zip(v, north, here)]
    return u, [v[0], v[1], jnp.where(last, 0.0, v[2])]


def by_level(row):
    return jnp.broadcast_to(row, (128, row.shape[1])).T


def level_constants(courant_row, c_mem):
    c = by_level(courant_row)
    c_mem[0] = c
    c_mem[1] = c * c
    c_mem[2] = 1.0 / c


def by_groups(work):
    def group(g, carry):
        work(pl.ds(pl.multiple_of(g * 8, 8), 8))
        return carry

    lax.fori_loop(0, LEVELS // 8, group, 0)
    work(slice(LEVELS // 8 * 8, LEVELS))


def silu(z):
    half = z * 0.5
    return half + half * jnp.tanh(half)


def normed_columns(state, gain, xs):
    columns = jnp.concatenate(
        [jnp.concatenate([f[x] for f in state], axis=0) for x in xs], axis=1
    )
    values = columns.astype(BF16).astype(F32)
    mean = jnp.sum(values * values, axis=0, keepdims=True) * (1.0 / ROWS)
    return (values * lax.rsqrt(mean + 1e-05) * gain).astype(BF16)


def network(normed, w1, b1, w2, b2, w3, h1, h2, beside=()):
    rows = normed.T
    for n in range(0, UNITS, TILE):
        z = lax.dot_general(rows, w1[:, n : n + TILE], NN, preferred_element_type=F32)
        h1[:, n : n + TILE] = silu(z + b1[:, n : n + TILE]).astype(BF16)
    for n in range(0, UNITS, TILE):
        z = lax.dot_general(h1[...], w2[:, n : n + TILE], NN, preferred_element_type=F32)
        h2[:, n : n + TILE] = silu(z + b2[:, n : n + TILE]).astype(BF16)
        if n // TILE < len(beside):
            beside[n // TILE]()
    t = lax.dot_general(h2[...], w3[...], NN, preferred_element_type=F32)
    return t.T.astype(BF16).astype(F32)


def keep_listed(t, mask, x):
    row = jnp.concatenate([mask[3 * x + j : 3 * x + j + 1, :] for j in range(3)], axis=1)
    return jnp.where(row > 0.5, t, 0.0)


def store_tendency(t, mask, xs, places, out):
    for i, (x, place) in enumerate(zip(xs, places)):
        listed = keep_listed(t[:, i * ACROSS : (i + 1) * ACROSS], mask, x)
        for f in range(3):
            out[place, f] = listed[f * LEVELS : (f + 1) * LEVELS]


WEIGHTS_SCRATCH = [
    pltpu.VMEM((ROWS, UNITS), BF16),
    pltpu.VMEM((1, UNITS), F32),
    pltpu.VMEM((UNITS, UNITS), BF16),
    pltpu.VMEM((1, UNITS), F32),
    pltpu.VMEM((ROWS, UNITS), BF16),
    pltpu.VMEM((UNITS, ROWS), BF16),
    pltpu.VMEM((CHUNK, UNITS), BF16),
    pltpu.VMEM((CHUNK, UNITS), BF16),
]


def network_flops(columns):
    return 2 * columns * (2 * ROWS * UNITS + UNITS * UNITS)


def interior_kernel(
    p_hbm, u_hbm, v_hbm, w1_hbm, b1_hbm, w2_hbm, b2_hbm, w3_hbm, courant, gain, lists,
    tend, mask,
    p_mem, u_mem, v_mem, a_mem, b_mem, d_mem, t_mem, c_mem, one_x, one_y,
    w1, b1, w2, b2, w3t, w3, h1, h2, sems,
):
    fields = run_copies([(p_hbm, p_mem), (u_hbm, u_mem), (v_hbm, v_mem)], sems)
    weights = run_copies([(w1_hbm, w1), (b1_hbm, b1), (w2_hbm, w2), (b2_hbm, b2),
                          (w3_hbm, w3t)], sems, 3)
    level_constants(courant[...], c_mem)
    gain_column = by_level(gain[...])[:, :1]
    for s in range(SLOTS):
        entry = lists[s]
        part, spot = entry >> 7, entry & 127
        where = slice(s * DEVICES, (s + 1) * DEVICES)
        one_x[:, where] = (
            lax.broadcasted_iota(jnp.int32, (48, DEVICES), 0) == part
        ).astype(F32).astype(BF16)
        one_y[:, where] = (
            lax.broadcasted_iota(jnp.int32, (128, DEVICES), 0) == spot
        ).astype(F32).astype(BF16)
    mask[...] = lax.dot_general(one_x[...], one_y[...], NT, preferred_element_type=F32)
    for copy in fields:
        copy.wait()

    def group(rows):
        c, square, inverse = (c_mem[i, rows, :] for i in range(3))

        def done(x, p, here, east):
            a_mem[x - 3, rows, :] = join(p)
            u, v = winds(split(u_mem[x, rows, :]), split(v_mem[x, rows, :]), c, here, east)
            b_mem[x - 3, rows, :] = join(u)
            d_mem[x - 3, rows, :] = join(v)

        def load_d(x):
            return own_divergence(split(u_mem[x, rows, :]), split(u_mem[x - 1, rows, :]),
                                  split(v_mem[x, rows, :]), inverse)

        march(3, 0, WIDTH - 1, square, lambda x: split(p_mem[x, rows, :]), load_d, done)

    by_groups(group)
    for copy in weights:
        copy.wait()
    w3[...] = w3t[...].T
    sent = []
    for i in range(3):
        xs = (2 * i, 2 * i + 1)
        t = network(normed_columns((a_mem, b_mem, d_mem), gain_column, xs), w1, b1, w2, b2, w3, h1, h2)
        store_tendency(t, mask, [x + 3 for x in xs], xs, t_mem)
        sent += run_copies([(t_mem.at[2 * i : 2 * i + 2], tend.at[2 * i : 2 * i + 2])], sems, 8 + i)
    for copy in sent:
        copy.wait()


def interior(p, u, v, weights, courant, gain, lists):
    column = pltpu.VMEM((WIDTH, LEVELS, ACROSS), F32)
    middle = pltpu.VMEM((WIDTH // 2, LEVELS, ACROSS), F32)
    return pl.pallas_call(
        interior_kernel,
        out_shape=(
            jax.ShapeDtypeStruct((WIDTH // 2, 3, LEVELS, ACROSS), F32),
            jax.ShapeDtypeStruct((48, 128), F32),
        ),
        in_specs=[ANY] * 8 + [VMEM] * 3,
        out_specs=(ANY, VMEM),
        scratch_shapes=[column] * 3 + [middle] * 3
        + [pltpu.VMEM((WIDTH // 2, 3, LEVELS, ACROSS), F32), pltpu.VMEM((3, LEVELS, 128), F32)]
        + [pltpu.VMEM((48, SLOTS * DEVICES), BF16), pltpu.VMEM((128, SLOTS * DEVICES), BF16)]
        + WEIGHTS_SCRATCH
        + [pltpu.SemaphoreType.DMA((11,))],
        compiler_params=pltpu.CompilerParams(vmem_limit_bytes=60 * 2**20),
        cost_estimate=pl.CostEstimate(
            flops=network_flops(WIDTH // 2 * ACROSS), bytes_accessed=8 * 2**20, transcendentals=0
        ),
        name="interior",
    )(p, u, v, *weights, courant, gain, lists)


def finish_kernel(
    p_hbm, u_hbm, v_hbm, left, right, tend, w1_hbm, b1_hbm, w2_hbm, b2_hbm, w3_hbm,
    mask, courant, gain,
    p_out, u_out, v_out,
    p_mem, u_mem, v_mem, e_mem, halo, a_mem, b_mem, d_mem, t_mem, c_mem, p_new, u_new, v_new,
    w1, b1, w2, b2, w3t, w3, h1, h2, sems,
):
    near, far = slice(0, HALO), slice(HALO, WIDTH)
    fields = run_copies(
        [
            (left, halo.at[0]),
            (p_hbm.at[near], p_mem.at[HALO : 2 * HALO]),
            (u_hbm.at[near], u_mem.at[near]),
            (v_hbm.at[near], v_mem.at[near]),
            (right, halo.at[1]),
            (p_hbm.at[far], p_mem.at[2 * HALO : 3 * HALO]),
            (u_hbm.at[far], u_mem.at[far]),
            (v_hbm.at[far], v_mem.at[far]),
        ],
        sems,
    )
    weights = run_copies([(w1_hbm, w1), (b1_hbm, b1), (w2_hbm, w2), (b2_hbm, b2),
                          (w3_hbm, w3t), (tend, t_mem.at[3:9])], sems, 8)
    level_constants(courant[...], c_mem)
    gain_column = by_level(gain[...])[:, :1]

    def loads(rows, inverse):
        def load_p(x):
            return split(p_mem[x + HALO, rows, :])

        def load_d(x):
            if x < 0:
                return [d * inverse for d in split(e_mem[x + HALO - 1, rows, :])]
            if x > WIDTH:
                return [d * inverse for d in split(e_mem[x - HALO, rows, :])]
            if x == WIDTH:
                return [(d - u) * inverse for d, u in zip(split(e_mem[HALO, rows, :]),
                                                          split(u_mem[WIDTH - 1, rows, :]))]
            west = u_mem[x - 1, rows, :] if x else e_mem[HALO - 1, rows, :]
            return own_divergence(split(u_mem[x, rows, :]), split(west),
                                  split(v_mem[x, rows, :]), inverse)

        return load_p, load_d

    def strip(start, low):
        def group(rows):
            c, square, inverse = (c_mem[i, rows, :] for i in range(3))

            def done(x, p, here, east):
                at = x - low - 3 + start
                a_mem[at, rows, :] = join(p)
                u, v = winds(split(u_mem[x, rows, :]), split(v_mem[x, rows, :]), c, here, east)
                b_mem[at, rows, :] = join(u)
                d_mem[at, rows, :] = join(v)

            march(3, low, low + 8, square, *loads(rows, inverse), done)

        by_groups(group)

    for copy in fields[:4]:
        copy.wait()
    for i in range(HALO):
        p_mem[i] = halo[0, i].astype(F32)
        e_mem[i] = halo[0, HALO + i].astype(F32)
    strip(0, -3)
    for copy in fields[4:]:
        copy.wait()
    for i in range(HALO):
        p_mem[HALO + WIDTH + i] = halo[1, i].astype(F32)
        e_mem[HALO + i] = halo[1, HALO + i].astype(F32)
    strip(3, 6)

    def dynamics(rows):
        c, square, inverse = (c_mem[i, rows, :] for i in range(3))

        def done(x, p, here, east):
            p_new[x, rows, :] = join(p)
            u, v = winds(split(u_mem[x, rows, :]), split(v_mem[x, rows, :]), c, here, east)
            u_new[x, rows, :] = join(u)
            v_new[x, rows, :] = join(v)

        march(6, -HALO, WIDTH + HALO - 1, square, *loads(rows, inverse), done)

    for copy in weights:
        copy.wait()
    w3[...] = w3t[...].T
    outs = []

    def send(low, high):
        for x in range(low, high):
            for f, new in enumerate((p_new, u_new, v_new)):
                new[x] = new[x] + t_mem[x, f]
        outs.extend(run_copies(
            [(new.at[low:high], out.at[low:high])
             for new, out in ((p_new, p_out), (u_new, u_out), (v_new, v_out))],
            sems, 3 * len(outs) // 3,
        ))

    columns = (0, 1, 2, 9, 10, 11)

    def groups(low, high):
        def run():
            for g in range(low, high):
                dynamics(pl.ds(8 * g, 8) if g < LEVELS // 8 else slice(LEVELS // 8 * 8, LEVELS))
        return run

    beside = (
        [groups(0, 1), groups(1, 2), groups(2, 3)],
        [groups(3, 4), groups(4, 5), groups(5, 6)],
        [groups(6, 7), groups(7, 8), lambda: send(0, 5), lambda: send(5, 10)],
    )
    for i in range(3):
        places = (2 * i, 2 * i + 1)
        xs = [columns[j] for j in places]
        t = network(normed_columns((a_mem, b_mem, d_mem), gain_column, places),
                    w1, b1, w2, b2, w3, h1, h2, beside[i])
        store_tendency(t, mask, xs, xs, t_mem)
    send(10, 12)
    for copy in outs:
        copy.wait()


def finish(p, u, v, left, right, tend, weights, mask, courant, gain):
    shape = jax.ShapeDtypeStruct((WIDTH, LEVELS, ACROSS), F32)
    column = pltpu.VMEM((WIDTH, LEVELS, ACROSS), F32)
    half = pltpu.VMEM((WIDTH // 2, LEVELS, ACROSS), F32)
    return pl.pallas_call(
        finish_kernel,
        out_shape=(shape,) * 3,
        in_specs=[ANY] * 11 + [VMEM] * 3,
        out_specs=(ANY,) * 3,
        scratch_shapes=[pltpu.VMEM((SPAN, LEVELS, ACROSS), F32)] + [column] * 3
        + [pltpu.VMEM((2, 2 * HALO, LEVELS, ACROSS), BF16)] + [half] * 3
        + [pltpu.VMEM((WIDTH, 3, LEVELS, ACROSS), F32), pltpu.VMEM((3, LEVELS, 128), F32)]
        + [column] * 3
        + WEIGHTS_SCRATCH
        + [pltpu.SemaphoreType.DMA((14,))],
        compiler_params=pltpu.CompilerParams(vmem_limit_bytes=60 * 2**20),
        cost_estimate=pl.CostEstimate(
            flops=network_flops(WIDTH // 2 * ACROSS), bytes_accessed=12 * 2**20, transcendentals=0
        ),
        name="finish",
    )(p, u, v, left, right, tend, *weights, mask, courant, gain)


def body(
    pressure, wind_x, wind_y, courant, send_list,
    norm_gain, w_first, b_first, w_second, b_second, w_last,
):
    p, u, v = [jnp.transpose(f, (1, 0, 2)) for f in (pressure, wind_x, wind_y)]
    courant, gain = courant.reshape(1, LEVELS), norm_gain.reshape(1, ROWS)
    lists = jnp.transpose(send_list, (2, 0, 1))
    weights = (w_first, b_first.reshape(1, UNITS), w_second, b_second.reshape(1, UNITS), w_last.T)
    to_next, to_prev = edges(p, u, v)
    left = lax.ppermute(to_next, AXES, [(i, (i + 1) % DEVICES) for i in range(DEVICES)])
    right = lax.ppermute(to_prev, AXES, [(i, (i - 1) % DEVICES) for i in range(DEVICES)])
    tend, mask = interior(p, u, v, weights, courant, gain, lists)
    outs = finish(p, u, v, left, right, tend, weights, mask, courant, gain)
    return tuple(jnp.transpose(f, (1, 0, 2)) for f in outs)


def solution(mesh):
    split = P(None, AXES, None)
    in_specs = (split,) * 3 + (P(), P(AXES, None, None)) + (P(),) * 6
    return jax.shard_map(
        body, mesh=mesh, in_specs=in_specs, out_specs=(split,) * 3, check_vma=False
    )
```

```python
import jax
import jax.numpy as jnp
from jax import lax
from jax.experimental import pallas as pl
from jax.experimental.pallas import tpu as pltpu
from jax.sharding import PartitionSpec as P

AXES = ("group", "tile")
LEVELS, WIDTH, ACROSS, UNITS, SLOTS, DEVICES = 60, 12, 384, 1024, 36, 128
ROWS = 3 * LEVELS
HALO = 6
SENT = 2 * HALO + 4
OPEN = pl.BlockSpec(memory_space=pl.ANY)
SPAN = WIDTH + 2 * HALO
CHUNK = 2 * ACROSS
TILE = 256
F32, BF16 = jnp.float32, jnp.bfloat16
NN = (((1,), (0,)), ((), ()))
NT = (((1,), (1,)), ((), ()))
ANY = pl.BlockSpec(memory_space=pltpu.HBM)
VMEM = pl.BlockSpec(memory_space=pltpu.VMEM)


def lanes(shape):
    return lax.broadcasted_iota(jnp.int32, shape, len(shape) - 1)


def split(value):
    return [value[:, i : i + 128] for i in range(0, ACROSS, 128)]


def join(parts):
    return jnp.concatenate(parts, axis=1)


def run_copies(pairs, sems, first=0):
    copies = [
        pltpu.make_async_copy(src, dst, sems.at[first + i]) for i, (src, dst) in enumerate(pairs)
    ]
    for copy in copies:
        copy.start()
    return copies


def divergence(v):
    v = jnp.where(lanes(v.shape) < ACROSS - 1, v, 0.0)
    return v - pltpu.roll(v, 1, 1)


def rest(value):
    return (value - value.astype(BF16).astype(F32)).astype(BF16)


def edges_kernel(p_hbm, u_hbm, v_hbm, to_next, to_prev, p_mem, u_mem, v_mem, r_mem, l_mem, sems):
    low, high = slice(0, HALO), slice(WIDTH - HALO, WIDTH)
    loads = run_copies(
        [(f.at[s], m.at[s]) for s in (high, low)
         for f, m in ((p_hbm, p_mem), (u_hbm, u_mem), (v_hbm, v_mem))],
        sems,
    )
    for copy in loads[:3]:
        copy.wait()
    for i in range(HALO):
        r_mem[i] = p_mem[WIDTH - HALO + i].astype(BF16)
    for i in range(HALO - 1):
        x = WIDTH - HALO + 1 + i
        div = (u_mem[x] - u_mem[x - 1]) + divergence(v_mem[x])
        r_mem[HALO + i] = div.astype(BF16)
        if x == WIDTH - 1:
            r_mem[2 * HALO + 2] = rest(div)
    r_mem[2 * HALO - 1] = u_mem[WIDTH - 1].astype(BF16)
    r_mem[2 * HALO] = rest(p_mem[WIDTH - 1])
    r_mem[2 * HALO + 1] = rest(p_mem[WIDTH - 2])
    r_mem[2 * HALO + 3] = rest(u_mem[WIDTH - 1])
    out_next = run_copies([(r_mem, to_next)], sems, 6)
    for copy in loads[3:]:
        copy.wait()
    for i in range(HALO):
        l_mem[i] = p_mem[i].astype(BF16)
    for x in range(HALO):
        west = u_mem[x - 1] if x else 0.0
        div = (u_mem[x] - west) + divergence(v_mem[x])
        l_mem[HALO + x] = div.astype(BF16)
        if x < 2:
            l_mem[2 * HALO + 2 + x] = rest(div)
    l_mem[2 * HALO] = rest(p_mem[0])
    l_mem[2 * HALO + 1] = rest(p_mem[1])
    for copy in out_next + run_copies([(l_mem, to_prev)], sems, 7):
        copy.wait()


def edges(p, u, v):
    shape = jax.ShapeDtypeStruct((SENT, LEVELS, ACROSS), BF16)
    return pl.pallas_call(
        edges_kernel,
        out_shape=(shape, shape),
        in_specs=[ANY] * 3,
        out_specs=(OPEN, OPEN),
        scratch_shapes=[pltpu.VMEM((WIDTH, LEVELS, ACROSS), F32)] * 3
        + [pltpu.VMEM((SENT, LEVELS, ACROSS), BF16)] * 2
        + [pltpu.SemaphoreType.DMA((8,))],
        compiler_params=pltpu.CompilerParams(vmem_limit_bytes=24 * 2**20),
        name="edges",
    )(p, u, v)


def march(count, low, high, square, load_p, load_d, done):
    ps = [{} for _ in range(count + 1)]
    ds = [{} for _ in range(count + 1)]
    sums = {}
    lane = lanes(square.shape)
    first, last = lane == 0, lane == 127

    def substep(k, x):
        west, here, east = (ps[k - 1][x + i] for i in (-1, 0, 1))
        down = [pltpu.roll(h, 127, 1) for h in here]
        up = [pltpu.roll(h, 1, 1) for h in here]
        north = [jnp.where(last, down[1], down[0]), jnp.where(last, down[2], down[1]),
                 jnp.where(last, here[2], down[2])]
        south = [jnp.where(first, here[0], up[0]), jnp.where(first, up[0], up[1]),
                 jnp.where(first, up[1], up[2])]
        ds[k][x] = [d - (((e + w) + (n + s)) - 4.0 * h)
                    for d, e, w, n, s, h in zip(ds[k - 1][x], east, west, north, south, here)]
        ps[k][x] = [h - square * d for h, d in zip(here, ds[k][x])]
        if k == count:
            done(x, ps[k][x], ds[k][x], sums[x], sums[x + 1])
        elif low + count - 1 <= x <= high - count + 1:
            sums[x] = [s + p for s, p in zip(sums[x], ps[k][x])]

    for t in range(low, high + 2 * count + 1):
        if t <= high:
            ps[0][t] = load_p(t)
            if low + count - 1 <= t <= high - count + 1:
                sums[t] = ps[0][t]
            if low < t < high:
                ds[0][t] = load_d(t)
        for k in range(1, count + 1):
            x = t - 2 * k
            if low + k <= x <= high - k:
                substep(k, x)


def own_divergence(u, west, v, inverse):
    lane = lanes(inverse.shape)
    first, last = lane == 0, lane == 127
    v = [v[0], v[1], jnp.where(last, 0.0, v[2])]
    up = [pltpu.roll(a, 1, 1) for a in v]
    south = [jnp.where(first, up[i - 1], up[i]) for i in range(3)]
    return [((a - w) + (b - s)) * inverse for a, w, b, s in zip(u, west, v, south)]


def winds(u, v, c, here, east):
    last = lanes(c.shape) == 127
    down = [pltpu.roll(s, 127, 1) for s in here]
    north = [jnp.where(last, down[1], down[0]), jnp.where(last, down[2], down[1]), down[2]]
    u = [a - c * (e - s) for a, e, s in zip(u, east, here)]
    v = [a - c * (n - s) for a, n, s in zip(v, north, here)]
    return u, [v[0], v[1], jnp.where(last, 0.0, v[2])]


def by_level(row):
    return jnp.broadcast_to(row, (128, row.shape[1])).T


def level_constants(courant_row, c_mem):
    c = by_level(courant_row)
    c_mem[0] = c
    c_mem[1] = c * c
    c_mem[2] = 1.0 / c


def group_rows(g):
    return pl.ds(8 * g, 8) if g < LEVELS // 8 else slice(LEVELS // 8 * 8, LEVELS)


def by_groups(work):
    def group(g, carry):
        work(pl.ds(pl.multiple_of(g * 8, 8), 8))
        return carry

    lax.fori_loop(0, LEVELS // 8, group, 0)
    work(group_rows(LEVELS // 8))


def silu(z):
    half = z * 0.5
    return half + half * jnp.tanh(half)


def normed_rows(read, gain, xs):
    columns = jnp.concatenate([jnp.concatenate(read(x), axis=0) for x in xs], axis=1)
    values = columns.astype(BF16).astype(F32)
    mean = jnp.sum(values * values, axis=0, keepdims=True) * (1.0 / ROWS)
    return (values * lax.rsqrt(mean + 1e-05) * gain).astype(BF16).T


def network(rows, w1, b1, w2, b2, w3, h1, h2, raw, beside=()):
    for n in range(0, UNITS, TILE):
        z = lax.dot_general(rows[...], w1[:, n : n + TILE], NN, preferred_element_type=F32)
        h1[:, n : n + TILE] = silu(z + b1[:, n : n + TILE]).astype(BF16)
    for n in range(0, UNITS, TILE):
        z = lax.dot_general(h1[...], w2[:, n : n + TILE], NN, preferred_element_type=F32)
        h2[:, n : n + TILE] = silu(z + b2[:, n : n + TILE]).astype(BF16)
        if n // TILE < len(beside):
            beside[n // TILE]()
    raw[...] = lax.dot_general(h2[...], w3[...], NN, preferred_element_type=F32)


def store_tendency(raw, mask, xs, places, out):
    t = raw[...].T.astype(BF16).astype(F32)
    for i, (x, place) in enumerate(zip(xs, places)):
        row = jnp.concatenate([mask[3 * x + j : 3 * x + j + 1, :] for j in range(3)], axis=1)
        listed = jnp.where(row > 0.5, t[:, i * ACROSS : (i + 1) * ACROSS], 0.0)
        for f in range(3):
            out[place, f] = listed[f * LEVELS : (f + 1) * LEVELS]


WEIGHTS_SCRATCH = [
    pltpu.VMEM((ROWS, UNITS), BF16),
    pltpu.VMEM((1, UNITS), F32),
    pltpu.VMEM((UNITS, UNITS), BF16),
    pltpu.VMEM((1, UNITS), F32),
    pltpu.VMEM((ROWS, UNITS), BF16),
    pltpu.VMEM((UNITS, ROWS), BF16),
    pltpu.VMEM((CHUNK, UNITS), BF16),
    pltpu.VMEM((CHUNK, UNITS), BF16),
    pltpu.VMEM((3, CHUNK, ROWS), BF16),
    pltpu.VMEM((3, CHUNK, ROWS), F32),
]


def network_flops(columns):
    return 2 * columns * (2 * ROWS * UNITS + UNITS * UNITS)


def interior_kernel(
    p_hbm, u_hbm, v_hbm, w1_hbm, b1_hbm, w2_hbm, b2_hbm, w3_hbm, courant, gain, lists,
    tend, mid, mask,
    p_mem, u_mem, v_mem, m_mem, t_mem, c_mem, one_x, one_y,
    w1, b1, w2, b2, w3t, w3, h1, h2, rows_mem, raw, sems,
):
    near, far = slice(0, 8), slice(8, WIDTH)
    fields = run_copies(
        [(f.at[s], m.at[s]) for s in (near, far)
         for f, m in ((p_hbm, p_mem), (u_hbm, u_mem), (v_hbm, v_mem))],
        sems,
    )
    weights = run_copies([(w3_hbm, w3t), (w1_hbm, w1), (b1_hbm, b1), (w2_hbm, w2), (b2_hbm, b2)],
                         sems, 6)
    level_constants(courant[...], c_mem)
    gain_column = by_level(gain[...])[:, :1]
    for s in range(SLOTS):
        entry = lists[s]
        part, spot = entry >> 7, entry & 127
        where = slice(s * DEVICES, (s + 1) * DEVICES)
        one_x[:, where] = (
            lax.broadcasted_iota(jnp.int32, (48, DEVICES), 0) == part
        ).astype(F32).astype(BF16)
        one_y[:, where] = (
            lax.broadcasted_iota(jnp.int32, (128, DEVICES), 0) == spot
        ).astype(F32).astype(BF16)
    mask[...] = lax.dot_general(one_x[...], one_y[...], NT, preferred_element_type=F32)

    def pair(i):
        def group(rows):
            c, square, inverse = (c_mem[j, rows, :] for j in range(3))

            def done(x, p, d, here, east):
                u, v = winds(split(u_mem[x, rows, :]), split(v_mem[x, rows, :]), c, here, east)
                for f, value in enumerate((p, u, v)):
                    m_mem[f, x - 3, rows, :] = join(value)

            def load_d(x):
                return own_divergence(split(u_mem[x, rows, :]), split(u_mem[x - 1, rows, :]),
                                      split(v_mem[x, rows, :]), inverse)

            march(3, 2 * i, 2 * i + 7, square, lambda x: split(p_mem[x, rows, :]), load_d, done)

        return group

    def read(x):
        return [m_mem[f, x] for f in range(3)]

    def prepare(i):
        rows_mem[i] = normed_rows(read, gain_column, (2 * i, 2 * i + 1))

    sent = []

    def post(i):
        xs = (2 * i, 2 * i + 1)
        store_tendency(raw.at[i], mask, [x + 3 for x in xs], xs, t_mem)
        sent.extend(run_copies([(t_mem.at[2 * i : 2 * i + 2], tend.at[2 * i : 2 * i + 2])],
                               sems, 11 + i))

    def some(i, low, high):
        def run():
            for g in range(low, high):
                pair(i)(group_rows(g))
        return run

    def both(*works):
        def run():
            for work in works:
                work()
        return run

    for copy in fields[:3]:
        copy.wait()
    by_groups(pair(0))
    for copy in fields[3:]:
        copy.wait()
    prepare(0)
    for copy in weights:
        copy.wait()
    w3[...] = w3t[...].T
    beside = (
        [some(1, 0, 3), some(1, 3, 6), both(some(1, 6, 8), some(2, 0, 1)),
         both(lambda: prepare(1), some(2, 1, 2))],
        [both(some(2, 2, 4), lambda: post(0)), some(2, 4, 6), some(2, 6, 8),
         lambda: prepare(2)],
        [lambda: sent.extend(run_copies([(m_mem, mid)], sems, 14)), lambda: post(1)],
    )
    for i in range(3):
        network(rows_mem.at[i], w1, b1, w2, b2, w3, h1, h2, raw.at[i], beside[i])
    post(2)
    for copy in sent:
        copy.wait()


def interior(p, u, v, weights, courant, gain, lists):
    column = pltpu.VMEM((WIDTH, LEVELS, ACROSS), F32)
    return pl.pallas_call(
        interior_kernel,
        out_shape=(
            jax.ShapeDtypeStruct((WIDTH // 2, 3, LEVELS, ACROSS), F32),
            jax.ShapeDtypeStruct((3, WIDTH // 2, LEVELS, ACROSS), F32),
            jax.ShapeDtypeStruct((48, 128), F32),
        ),
        in_specs=[ANY] * 8 + [VMEM] * 3,
        out_specs=(ANY, ANY, VMEM),
        scratch_shapes=[column] * 3
        + [pltpu.VMEM((3, WIDTH // 2, LEVELS, ACROSS), F32)]
        + [pltpu.VMEM((WIDTH // 2, 3, LEVELS, ACROSS), F32), pltpu.VMEM((3, LEVELS, 128), F32)]
        + [pltpu.VMEM((48, SLOTS * DEVICES), BF16), pltpu.VMEM((128, SLOTS * DEVICES), BF16)]
        + WEIGHTS_SCRATCH
        + [pltpu.SemaphoreType.DMA((15,))],
        compiler_params=pltpu.CompilerParams(vmem_limit_bytes=52 * 2**20),
        cost_estimate=pl.CostEstimate(
            flops=network_flops(WIDTH // 2 * ACROSS), bytes_accessed=8 * 2**20, transcendentals=0
        ),
        name="interior",
    )(p, u, v, *weights, courant, gain, lists)


def finish_kernel(
    p_hbm, u_hbm, v_hbm, left, right, tend, mid, w1_hbm, b1_hbm, w2_hbm, b2_hbm, w3_hbm,
    mask, courant, gain,
    p_out, u_out, v_out,
    p_mem, u_mem, v_mem, e_mem, halo, a_mem, b_mem, d_mem, g_mem, t_mem, c_mem,
    p_new, u_new, v_new,
    w1, b1, w2, b2, w3t, w3, h1, h2, rows_mem, raw, sems,
):
    near, far = slice(0, HALO), slice(HALO, WIDTH)
    fields = run_copies(
        [
            (left, halo.at[0]),
            (p_hbm.at[near], p_mem.at[HALO : 2 * HALO]),
            (u_hbm.at[near], u_mem.at[near]),
            (v_hbm.at[near], v_mem.at[near]),
            (right, halo.at[1]),
            (p_hbm.at[far], p_mem.at[2 * HALO : 3 * HALO]),
            (u_hbm.at[far], u_mem.at[far]),
            (v_hbm.at[far], v_mem.at[far]),
        ],
        sems,
    )
    weights = run_copies(
        [(w3_hbm, w3t), (w1_hbm, w1), (b1_hbm, b1), (w2_hbm, w2), (b2_hbm, b2),
         (mid.at[0], a_mem.at[6:12]), (mid.at[1], b_mem.at[3:9]), (mid.at[2], d_mem.at[3:9]),
         (tend, t_mem.at[3:9])],
        sems, 8,
    )
    level_constants(courant[...], c_mem)
    gain_column = by_level(gain[...])[:, :1]

    def loads(rows, inverse):
        def load_p(x):
            return split(p_mem[x + HALO, rows, :])

        def load_d(x):
            if x < 0:
                return [d * inverse for d in split(e_mem[x + HALO - 1, rows, :])]
            if x > WIDTH:
                return [d * inverse for d in split(e_mem[x - HALO, rows, :])]
            if x == WIDTH:
                return [(d - u) * inverse for d, u in zip(split(e_mem[HALO, rows, :]),
                                                          split(u_mem[WIDTH - 1, rows, :]))]
            west = u_mem[x - 1, rows, :] if x else e_mem[HALO - 1, rows, :]
            return own_divergence(split(u_mem[x, rows, :]), split(west),
                                  split(v_mem[x, rows, :]), inverse)

        return load_p, load_d

    def strip(low):
        def group(rows):
            c, square, inverse = (c_mem[i, rows, :] for i in range(3))

            def done(x, p, d, here, east):
                a_mem[x + 3, rows, :] = join(p)
                u, v = winds(split(u_mem[x, rows, :]), split(v_mem[x, rows, :]), c, here, east)
                b_mem[x, rows, :] = join(u)
                d_mem[x, rows, :] = join(v)
                if x == 0:
                    g_mem[3, rows, :] = join(d)

            march(3, low, low + 8, square, *loads(rows, inverse), done)

        by_groups(group)

    for copy in fields[:4]:
        copy.wait()
    for i in range(HALO):
        p_mem[i] = halo[0, i].astype(F32)
        e_mem[i] = halo[0, HALO + i].astype(F32)
    p_mem[HALO - 1] = p_mem[HALO - 1] + halo[0, 2 * HALO].astype(F32)
    p_mem[HALO - 2] = p_mem[HALO - 2] + halo[0, 2 * HALO + 1].astype(F32)
    e_mem[HALO - 2] = e_mem[HALO - 2] + halo[0, 2 * HALO + 2].astype(F32)
    e_mem[HALO - 1] = e_mem[HALO - 1] + halo[0, 2 * HALO + 3].astype(F32)
    strip(-3)
    for copy in fields[4:]:
        copy.wait()
    for i in range(HALO):
        p_mem[HALO + WIDTH + i] = halo[1, i].astype(F32)
        e_mem[HALO + i] = halo[1, HALO + i].astype(F32)
    for i in range(2):
        p_mem[HALO + WIDTH + i] = p_mem[HALO + WIDTH + i] + halo[1, 2 * HALO + i].astype(F32)
        e_mem[HALO + i] = e_mem[HALO + i] + halo[1, 2 * HALO + 2 + i].astype(F32)
    strip(6)

    def dynamics(g):
        rows = group_rows(g)
        c, square, inverse = (c_mem[i, rows, :] for i in range(3))

        def outer(x, p, d, here, east):
            a_mem[x + 3, rows, :] = join(p)
            g_mem[x + 3 if x < 0 else x - 8, rows, :] = join(d)

        march(3, -6, 2, square, *loads(rows, inverse), outer)
        march(3, 9, 17, square, *loads(rows, inverse), outer)

        def load_d(x):
            if 0 < x < WIDTH:
                return own_divergence(split(b_mem[x, rows, :]), split(b_mem[x - 1, rows, :]),
                                      split(d_mem[x, rows, :]), inverse)
            return split(g_mem[x + 3 if x <= 0 else x - 8, rows, :])

        def done(x, p, d, here, east):
            p_new[x, rows, :] = join(p)
            u, v = winds(split(b_mem[x, rows, :]), split(d_mem[x, rows, :]), c, here, east)
            u_new[x, rows, :] = join(u)
            v_new[x, rows, :] = join(v)

        march(3, -3, 14, square, lambda x: split(a_mem[x + 3, rows, :]), load_d, done)

    columns = (0, 1, 2, 9, 10, 11)

    def read(x):
        return a_mem[x + 3], b_mem[x], d_mem[x]

    def prepare(i):
        rows_mem[i] = normed_rows(read, gain_column, columns[2 * i : 2 * i + 2])

    def post(i):
        xs = columns[2 * i : 2 * i + 2]
        store_tendency(raw.at[i], mask, xs, xs, t_mem)

    outs = []

    def send(low, high):
        for x in range(low, high):
            for f, new in enumerate((p_new, u_new, v_new)):
                new[x] = new[x] + t_mem[x, f]
        outs.extend(run_copies(
            [(new.at[low:high], out.at[low:high])
             for new, out in ((p_new, p_out), (u_new, u_out), (v_new, v_out))],
            sems, len(outs),
        ))

    def both(*works):
        def run():
            for work in works:
                work()
        return run

    def group(g):
        return lambda: dynamics(g)

    prepare(0)
    for copy in weights:
        copy.wait()
    w3[...] = w3t[...].T
    beside = (
        [group(0), group(1), group(2), lambda: prepare(1)],
        [group(3), group(4), group(5), both(lambda: prepare(2), lambda: post(0))],
        [group(6), group(7), both(lambda: post(1), lambda: send(0, 4)), lambda: send(4, 10)],
    )
    for i in range(3):
        network(rows_mem.at[i], w1, b1, w2, b2, w3, h1, h2, raw.at[i], beside[i])
    post(2)
    send(10, 12)
    for copy in outs:
        copy.wait()


def finish(p, u, v, left, right, tend, mid, weights, mask, courant, gain):
    shape = jax.ShapeDtypeStruct((WIDTH, LEVELS, ACROSS), F32)
    column = pltpu.VMEM((WIDTH, LEVELS, ACROSS), F32)
    return pl.pallas_call(
        finish_kernel,
        out_shape=(shape,) * 3,
        in_specs=[ANY] * 3 + [OPEN] * 2 + [ANY] * 7 + [VMEM] * 3,
        out_specs=(ANY,) * 3,
        scratch_shapes=[pltpu.VMEM((SPAN, LEVELS, ACROSS), F32)] + [column] * 3
        + [pltpu.VMEM((2, SENT, LEVELS, ACROSS), BF16)]
        + [pltpu.VMEM((WIDTH + 6, LEVELS, ACROSS), F32), column, column]
        + [pltpu.VMEM((7, LEVELS, ACROSS), F32)]
        + [pltpu.VMEM((WIDTH, 3, LEVELS, ACROSS), F32), pltpu.VMEM((3, LEVELS, 128), F32)]
        + [column] * 3
        + WEIGHTS_SCRATCH
        + [pltpu.SemaphoreType.DMA((17,))],
        compiler_params=pltpu.CompilerParams(vmem_limit_bytes=52 * 2**20),
        cost_estimate=pl.CostEstimate(
            flops=network_flops(WIDTH // 2 * ACROSS), bytes_accessed=12 * 2**20, transcendentals=0
        ),
        name="finish",
    )(p, u, v, left, right, tend, mid, *weights, mask, courant, gain)


def body(
    pressure, wind_x, wind_y, courant, send_list,
    norm_gain, w_first, b_first, w_second, b_second, w_last,
):
    p, u, v = [jnp.transpose(f, (1, 0, 2)) for f in (pressure, wind_x, wind_y)]
    courant, gain = courant.reshape(1, LEVELS), norm_gain.reshape(1, ROWS)
    lists = jnp.transpose(send_list, (2, 0, 1))
    weights = (w_first, b_first.reshape(1, UNITS), w_second, b_second.reshape(1, UNITS), w_last.T)
    to_next, to_prev = edges(p, u, v)
    left = lax.ppermute(to_next, AXES, [(i, (i + 1) % DEVICES) for i in range(DEVICES)])
    right = lax.ppermute(to_prev, AXES, [(i, (i - 1) % DEVICES) for i in range(DEVICES)])
    tend, mid, mask = interior(p, u, v, weights, courant, gain, lists)
    outs = finish(p, u, v, left, right, tend, mid, weights, mask, courant, gain)
    return tuple(jnp.transpose(f, (1, 0, 2)) for f in outs)


def solution(mesh):
    split = P(None, AXES, None)
    in_specs = (split,) * 3 + (P(), P(AXES, None, None)) + (P(),) * 6
    return jax.shard_map(
        body, mesh=mesh, in_specs=in_specs, out_specs=(split,) * 3, check_vma=False
    )
```

```python
import jax
import jax.numpy as jnp
from jax import lax
from jax.experimental import pallas as pl
from jax.experimental.pallas import tpu as pltpu
from jax.sharding import PartitionSpec as P

AXES = ("group", "tile")
LEVELS, WIDTH, ACROSS, UNITS, SLOTS, DEVICES = 60, 12, 384, 1024, 36, 128
ROWS = 3 * LEVELS
HALO = 6
SENT = 3 * HALO
OPEN = pl.BlockSpec(memory_space=pl.ANY)
SPAN = WIDTH + 2 * HALO
CHUNK = 2 * ACROSS
TILE = 256
F32, BF16 = jnp.float32, jnp.bfloat16
NN = (((1,), (0,)), ((), ()))
NT = (((1,), (1,)), ((), ()))
ANY = pl.BlockSpec(memory_space=pltpu.HBM)
VMEM = pl.BlockSpec(memory_space=pltpu.VMEM)


def lanes(shape):
    return lax.broadcasted_iota(jnp.int32, shape, len(shape) - 1)


def split(value):
    return [value[:, i : i + 128] for i in range(0, ACROSS, 128)]


def join(parts):
    return jnp.concatenate(parts, axis=1)


def run_copies(pairs, sems, first=0):
    copies = [
        pltpu.make_async_copy(src, dst, sems.at[first + i]) for i, (src, dst) in enumerate(pairs)
    ]
    for copy in copies:
        copy.start()
    return copies


def divergence(v):
    v = jnp.where(lanes(v.shape) < ACROSS - 1, v, 0.0)
    return v - pltpu.roll(v, 1, 1)


def rest(value):
    return (value - value.astype(BF16).astype(F32)).astype(BF16)


def edges_kernel(p_hbm, u_hbm, v_hbm, to_next, to_prev, p_mem, u_mem, v_mem, r_mem, l_mem, sems):
    low, high = slice(0, HALO), slice(WIDTH - HALO, WIDTH)
    loads = run_copies(
        [(f.at[s], m.at[s]) for s in (high, low)
         for f, m in ((p_hbm, p_mem), (u_hbm, u_mem), (v_hbm, v_mem))],
        sems,
    )
    for copy in loads[:3]:
        copy.wait()
    for i in range(HALO):
        r_mem[i] = p_mem[WIDTH - HALO + i].astype(BF16)
    for i in range(HALO - 1):
        x = WIDTH - HALO + 1 + i
        div = (u_mem[x] - u_mem[x - 1]) + divergence(v_mem[x])
        r_mem[HALO + i] = div.astype(BF16)
        if x >= WIDTH - 2:
            r_mem[2 * HALO + 2 + WIDTH - x] = rest(div)
    r_mem[2 * HALO - 1] = u_mem[WIDTH - 1].astype(BF16)
    for i in range(3):
        r_mem[2 * HALO + i] = rest(p_mem[WIDTH - 1 - i])
    r_mem[SENT - 1] = rest(u_mem[WIDTH - 1])
    out_next = run_copies([(r_mem, to_next)], sems, 6)
    for copy in loads[3:]:
        copy.wait()
    for i in range(HALO):
        l_mem[i] = p_mem[i].astype(BF16)
    for x in range(HALO):
        west = u_mem[x - 1] if x else 0.0
        div = (u_mem[x] - west) + divergence(v_mem[x])
        l_mem[HALO + x] = div.astype(BF16)
        if x < 3:
            l_mem[2 * HALO + 3 + x] = rest(div)
    for i in range(3):
        l_mem[2 * HALO + i] = rest(p_mem[i])
    for copy in out_next + run_copies([(l_mem, to_prev)], sems, 7):
        copy.wait()


def edges(p, u, v):
    shape = jax.ShapeDtypeStruct((SENT, LEVELS, ACROSS), BF16)
    return pl.pallas_call(
        edges_kernel,
        out_shape=(shape, shape),
        in_specs=[ANY] * 3,
        out_specs=(OPEN, OPEN),
        scratch_shapes=[pltpu.VMEM((WIDTH, LEVELS, ACROSS), F32)] * 3
        + [pltpu.VMEM((SENT, LEVELS, ACROSS), BF16)] * 2
        + [pltpu.SemaphoreType.DMA((8,))],
        compiler_params=pltpu.CompilerParams(vmem_limit_bytes=60 * 2**20),
        name="edges",
    )(p, u, v)


def stepping(count, low, high, square, load_p, load_d, done):
    ps = [{} for _ in range(count + 1)]
    ds = [{} for _ in range(count + 1)]
    sums = {}
    lane = lanes(square.shape)
    first, last = lane == 0, lane == 127

    def substep(k, x):
        west, here, east = (ps[k - 1][x + i] for i in (-1, 0, 1))
        down = [pltpu.roll(h, 127, 1) for h in here]
        up = [pltpu.roll(h, 1, 1) for h in here]
        north = [jnp.where(last, down[1], down[0]), jnp.where(last, down[2], down[1]),
                 jnp.where(last, here[2], down[2])]
        south = [jnp.where(first, here[0], up[0]), jnp.where(first, up[0], up[1]),
                 jnp.where(first, up[1], up[2])]
        ds[k][x] = [d - (((e + w) + (n + s)) - 4.0 * h)
                    for d, e, w, n, s, h in zip(ds[k - 1][x], east, west, north, south, here)]
        ps[k][x] = [h - square * d for h, d in zip(here, ds[k][x])]
        if k == count:
            done(x, ps[k][x], ds[k][x], sums[x], sums[x + 1])
        elif low + count - 1 <= x <= high - count + 1:
            sums[x] = [s + p for s, p in zip(sums[x], ps[k][x])]

    for t in range(low, high + 2 * count + 1):
        if t <= high:
            ps[0][t] = load_p(t)
            if low + count - 1 <= t <= high - count + 1:
                sums[t] = ps[0][t]
            if low < t < high:
                ds[0][t] = load_d(t)
        for k in range(1, count + 1):
            x = t - 2 * k
            if low + k <= x <= high - k:
                substep(k, x)
        yield


def march(*args):
    for _ in stepping(*args):
        pass


def march_both(one, two):
    for _ in zip(stepping(*one), stepping(*two), strict=True):
        pass


def own_divergence(u, west, v, inverse):
    lane = lanes(inverse.shape)
    first, last = lane == 0, lane == 127
    v = [v[0], v[1], jnp.where(last, 0.0, v[2])]
    up = [pltpu.roll(a, 1, 1) for a in v]
    south = [jnp.where(first, up[i - 1], up[i]) for i in range(3)]
    return [((a - w) + (b - s)) * inverse for a, w, b, s in zip(u, west, v, south)]


def winds(u, v, c, here, east):
    last = lanes(c.shape) == 127
    down = [pltpu.roll(s, 127, 1) for s in here]
    north = [jnp.where(last, down[1], down[0]), jnp.where(last, down[2], down[1]), down[2]]
    u = [a - c * (e - s) for a, e, s in zip(u, east, here)]
    v = [a - c * (n - s) for a, n, s in zip(v, north, here)]
    return u, [v[0], v[1], jnp.where(last, 0.0, v[2])]


def by_level(row):
    return jnp.broadcast_to(row, (128, row.shape[1])).T


def level_constants(courant_row, c_mem):
    c = by_level(courant_row)
    c_mem[0] = c
    c_mem[1] = c * c
    c_mem[2] = 1.0 / c


def group_rows(g):
    return pl.ds(8 * g, 8) if g < LEVELS // 8 else slice(LEVELS // 8 * 8, LEVELS)


def by_groups(work):
    def group(g, carry):
        work(pl.ds(pl.multiple_of(g * 8, 8), 8))
        return carry

    lax.fori_loop(0, LEVELS // 8, group, 0)
    work(group_rows(LEVELS // 8))


def silu(z):
    half = z * 0.5
    return half + half * jnp.tanh(half)


def normed_rows(read, gain, xs):
    columns = jnp.concatenate([jnp.concatenate(read(x), axis=0) for x in xs], axis=1)
    values = columns.astype(BF16).astype(F32)
    mean = jnp.sum(values * values, axis=0, keepdims=True) * (1.0 / ROWS)
    return (values * lax.rsqrt(mean + 1e-05) * gain).astype(BF16).T


def network(rows, w1, b1, w2, b2, w3, h1, h2, raw, beside=()):
    for n in range(0, UNITS, TILE):
        z = lax.dot_general(rows[...], w1[:, n : n + TILE], NN, preferred_element_type=F32)
        h1[:, n : n + TILE] = silu(z + b1[:, n : n + TILE]).astype(BF16)
    for n in range(0, UNITS, TILE):
        z = lax.dot_general(h1[...], w2[:, n : n + TILE], NN, preferred_element_type=F32)
        h2[:, n : n + TILE] = silu(z + b2[:, n : n + TILE]).astype(BF16)
        if n // TILE < len(beside):
            beside[n // TILE]()
    raw[...] = lax.dot_general(h2[...], w3[...], NN, preferred_element_type=F32)


def store_tendency(raw, mask, xs, places, out):
    t = raw[...].T.astype(BF16).astype(F32)
    for i, (x, place) in enumerate(zip(xs, places)):
        row = jnp.concatenate([mask[3 * x + j : 3 * x + j + 1, :] for j in range(3)], axis=1)
        listed = jnp.where(row > 0.5, t[:, i * ACROSS : (i + 1) * ACROSS], 0.0)
        for f in range(3):
            out[place, f] = listed[f * LEVELS : (f + 1) * LEVELS]


WEIGHTS_SCRATCH = [
    pltpu.VMEM((ROWS, UNITS), BF16),
    pltpu.VMEM((1, UNITS), F32),
    pltpu.VMEM((UNITS, UNITS), BF16),
    pltpu.VMEM((1, UNITS), F32),
    pltpu.VMEM((ROWS, UNITS), BF16),
    pltpu.VMEM((UNITS, ROWS), BF16),
    pltpu.VMEM((CHUNK, UNITS), BF16),
    pltpu.VMEM((CHUNK, UNITS), BF16),
    pltpu.VMEM((3, CHUNK, ROWS), BF16),
    pltpu.VMEM((3, CHUNK, ROWS), F32),
]


def network_flops(columns):
    return 2 * columns * (2 * ROWS * UNITS + UNITS * UNITS)


def interior_kernel(
    p_hbm, u_hbm, v_hbm, w1_hbm, b1_hbm, w2_hbm, b2_hbm, w3_hbm, courant, gain, lists,
    tend, mid, mask,
    p_mem, u_mem, v_mem, m_mem, t_mem, c_mem, one_x, one_y,
    w1, b1, w2, b2, w3t, w3, h1, h2, rows_mem, raw, sems,
):
    near, far = slice(0, 8), slice(8, WIDTH)
    fields = run_copies(
        [(f.at[s], m.at[s]) for s in (near, far)
         for f, m in ((p_hbm, p_mem), (u_hbm, u_mem), (v_hbm, v_mem))],
        sems,
    )
    weights = run_copies([(w3_hbm, w3t), (w1_hbm, w1), (b1_hbm, b1), (w2_hbm, w2), (b2_hbm, b2)],
                         sems, 6)
    level_constants(courant[...], c_mem)
    gain_column = by_level(gain[...])[:, :1]
    for s in range(SLOTS):
        entry = lists[s]
        part, spot = entry >> 7, entry & 127
        where = slice(s * DEVICES, (s + 1) * DEVICES)
        one_x[:, where] = (
            lax.broadcasted_iota(jnp.int32, (48, DEVICES), 0) == part
        ).astype(F32).astype(BF16)
        one_y[:, where] = (
            lax.broadcasted_iota(jnp.int32, (128, DEVICES), 0) == spot
        ).astype(F32).astype(BF16)
    mask[...] = lax.dot_general(one_x[...], one_y[...], NT, preferred_element_type=F32)

    def pair(i):
        def group(rows):
            c, square, inverse = (c_mem[j, rows, :] for j in range(3))

            def done(x, p, d, here, east):
                u, v = winds(split(u_mem[x, rows, :]), split(v_mem[x, rows, :]), c, here, east)
                for f, value in enumerate((p, u, v)):
                    m_mem[f, x - 3, rows, :] = join(value)

            def load_d(x):
                return own_divergence(split(u_mem[x, rows, :]), split(u_mem[x - 1, rows, :]),
                                      split(v_mem[x, rows, :]), inverse)

            march(3, 2 * i, 2 * i + 7, square, lambda x: split(p_mem[x, rows, :]), load_d, done)

        return group

    def read(x):
        return [m_mem[f, x] for f in range(3)]

    def prepare(i):
        rows_mem[i] = normed_rows(read, gain_column, (2 * i, 2 * i + 1))

    sent = []

    def post(i):
        xs = (2 * i, 2 * i + 1)
        store_tendency(raw.at[i], mask, [x + 3 for x in xs], xs, t_mem)
        sent.extend(run_copies([(t_mem.at[2 * i : 2 * i + 2], tend.at[2 * i : 2 * i + 2])],
                               sems, 11 + i))

    def some(i, low, high):
        def run():
            for g in range(low, high):
                pair(i)(group_rows(g))
        return run

    def both(*works):
        def run():
            for work in works:
                work()
        return run

    for copy in fields[:3]:
        copy.wait()
    by_groups(pair(0))
    for copy in fields[3:]:
        copy.wait()
    prepare(0)
    for copy in weights:
        copy.wait()
    w3[...] = w3t[...].T
    beside = (
        [some(1, 0, 3), some(1, 3, 6), both(some(1, 6, 8), some(2, 0, 1)),
         both(lambda: prepare(1), some(2, 1, 2))],
        [both(some(2, 2, 4), lambda: post(0)), some(2, 4, 6), some(2, 6, 8),
         lambda: prepare(2)],
        [lambda: sent.extend(run_copies([(m_mem, mid)], sems, 14)), lambda: post(1)],
    )
    for i in range(3):
        network(rows_mem.at[i], w1, b1, w2, b2, w3, h1, h2, raw.at[i], beside[i])
    post(2)
    for copy in sent:
        copy.wait()


def interior(p, u, v, weights, courant, gain, lists):
    column = pltpu.VMEM((WIDTH, LEVELS, ACROSS), F32)
    return pl.pallas_call(
        interior_kernel,
        out_shape=(
            jax.ShapeDtypeStruct((WIDTH // 2, 3, LEVELS, ACROSS), F32),
            jax.ShapeDtypeStruct((3, WIDTH // 2, LEVELS, ACROSS), F32),
            jax.ShapeDtypeStruct((48, 128), F32),
        ),
        in_specs=[ANY] * 8 + [VMEM] * 3,
        out_specs=(ANY, ANY, VMEM),
        scratch_shapes=[column] * 3
        + [pltpu.VMEM((3, WIDTH // 2, LEVELS, ACROSS), F32)]
        + [pltpu.VMEM((WIDTH // 2, 3, LEVELS, ACROSS), F32), pltpu.VMEM((3, LEVELS, 128), F32)]
        + [pltpu.VMEM((48, SLOTS * DEVICES), BF16), pltpu.VMEM((128, SLOTS * DEVICES), BF16)]
        + WEIGHTS_SCRATCH
        + [pltpu.SemaphoreType.DMA((15,))],
        compiler_params=pltpu.CompilerParams(vmem_limit_bytes=52 * 2**20),
        cost_estimate=pl.CostEstimate(
            flops=network_flops(WIDTH // 2 * ACROSS), bytes_accessed=8 * 2**20, transcendentals=0
        ),
        name="interior",
    )(p, u, v, *weights, courant, gain, lists)


def finish_kernel(
    p_hbm, u_hbm, v_hbm, left, right, tend, mid, w1_hbm, b1_hbm, w2_hbm, b2_hbm, w3_hbm,
    mask, courant, gain,
    p_out, u_out, v_out,
    p_mem, u_mem, v_mem, e_mem, halo, a_mem, b_mem, d_mem, g_mem, t_mem, c_mem,
    p_new, u_new, v_new,
    w1, b1, w2, b2, w3t, w3, h1, h2, rows_mem, raw, sems,
):
    near, far = slice(0, HALO), slice(HALO, WIDTH)
    fields = run_copies(
        [
            (left, halo.at[0]),
            (p_hbm.at[near], p_mem.at[HALO : 2 * HALO]),
            (u_hbm.at[near], u_mem.at[near]),
            (v_hbm.at[near], v_mem.at[near]),
            (right, halo.at[1]),
            (p_hbm.at[far], p_mem.at[2 * HALO : 3 * HALO]),
            (u_hbm.at[far], u_mem.at[far]),
            (v_hbm.at[far], v_mem.at[far]),
        ],
        sems,
    )

    def start_weights():
        return run_copies(
            [(w3_hbm, w3t), (w1_hbm, w1), (b1_hbm, b1), (w2_hbm, w2), (b2_hbm, b2),
             (mid.at[0], a_mem.at[6:12]), (mid.at[1], b_mem.at[3:9]), (mid.at[2], d_mem.at[3:9]),
             (tend, t_mem.at[3:9])],
            sems, 8,
        )

    level_constants(courant[...], c_mem)
    gain_column = by_level(gain[...])[:, :1]

    def loads(rows, inverse):
        def load_p(x):
            return split(p_mem[x + HALO, rows, :])

        def load_d(x):
            if x < 0:
                return [d * inverse for d in split(e_mem[x + HALO - 1, rows, :])]
            if x > WIDTH:
                return [d * inverse for d in split(e_mem[x - HALO, rows, :])]
            if x == WIDTH:
                return [(d - u) * inverse for d, u in zip(split(e_mem[HALO, rows, :]),
                                                          split(u_mem[WIDTH - 1, rows, :]))]
            west = u_mem[x - 1, rows, :] if x else e_mem[HALO - 1, rows, :]
            return own_divergence(split(u_mem[x, rows, :]), split(west),
                                  split(v_mem[x, rows, :]), inverse)

        return load_p, load_d

    def strips(rows):
        c, square, inverse = (c_mem[i, rows, :] for i in range(3))

        def done(x, p, d, here, east):
            a_mem[x + 3, rows, :] = join(p)
            u, v = winds(split(u_mem[x, rows, :]), split(v_mem[x, rows, :]), c, here, east)
            b_mem[x, rows, :] = join(u)
            d_mem[x, rows, :] = join(v)
            if x == 0:
                g_mem[3, rows, :] = join(d)

        common = (square, *loads(rows, inverse), done)
        march_both((3, -3, 5, *common), (3, 6, 14, *common))

    for copy in fields[:4]:
        copy.wait()
    for i in range(HALO):
        p_mem[i] = halo[0, i].astype(F32)
        e_mem[i] = halo[0, HALO + i].astype(F32)
    for i, (near_p, near_e) in enumerate(((1, 2), (2, 3), (3, 1))):
        p_mem[HALO - near_p] = p_mem[HALO - near_p] + halo[0, 2 * HALO + i].astype(F32)
        e_mem[HALO - near_e] = e_mem[HALO - near_e] + halo[0, 2 * HALO + 3 + i].astype(F32)
    for copy in fields[4:]:
        copy.wait()
    for i in range(HALO):
        p_mem[HALO + WIDTH + i] = halo[1, i].astype(F32)
        e_mem[HALO + i] = halo[1, HALO + i].astype(F32)
    for i in range(3):
        p_mem[HALO + WIDTH + i] = p_mem[HALO + WIDTH + i] + halo[1, 2 * HALO + i].astype(F32)
        e_mem[HALO + i] = e_mem[HALO + i] + halo[1, 2 * HALO + 3 + i].astype(F32)
    weights = start_weights()
    by_groups(strips)

    def dynamics(g):
        rows = group_rows(g)
        c, square, inverse = (c_mem[i, rows, :] for i in range(3))

        def outer(x, p, d, here, east):
            a_mem[x + 3, rows, :] = join(p)
            g_mem[x + 3 if x < 0 else x - 8, rows, :] = join(d)

        common = (square, *loads(rows, inverse), outer)
        march_both((3, -6, 2, *common), (3, 9, 17, *common))

        def load_d(x):
            if 0 < x < WIDTH:
                return own_divergence(split(b_mem[x, rows, :]), split(b_mem[x - 1, rows, :]),
                                      split(d_mem[x, rows, :]), inverse)
            return split(g_mem[x + 3 if x <= 0 else x - 8, rows, :])

        def done(x, p, d, here, east):
            p_new[x, rows, :] = join(p)
            u, v = winds(split(b_mem[x, rows, :]), split(d_mem[x, rows, :]), c, here, east)
            u_new[x, rows, :] = join(u)
            v_new[x, rows, :] = join(v)

        march(3, -3, 14, square, lambda x: split(a_mem[x + 3, rows, :]), load_d, done)

    columns = (0, 1, 2, 9, 10, 11)

    def read(x):
        return a_mem[x + 3], b_mem[x], d_mem[x]

    def prepare(i):
        rows_mem[i] = normed_rows(read, gain_column, columns[2 * i : 2 * i + 2])

    def post(i):
        xs = columns[2 * i : 2 * i + 2]
        store_tendency(raw.at[i], mask, xs, xs, t_mem)

    outs = []

    def send(low, high):
        for x in range(low, high):
            for f, new in enumerate((p_new, u_new, v_new)):
                new[x] = new[x] + t_mem[x, f]
        outs.extend(run_copies(
            [(new.at[low:high], out.at[low:high])
             for new, out in ((p_new, p_out), (u_new, u_out), (v_new, v_out))],
            sems, len(outs),
        ))

    def both(*works):
        def run():
            for work in works:
                work()
        return run

    def group(g):
        return lambda: dynamics(g)

    prepare(0)
    for copy in weights:
        copy.wait()
    w3[...] = w3t[...].T
    beside = (
        [group(0), group(1), group(2), lambda: prepare(1)],
        [group(3), group(4), group(5), both(lambda: prepare(2), lambda: post(0))],
        [group(6), group(7), both(lambda: post(1), lambda: send(0, 4)), lambda: send(4, 10)],
    )
    for i in range(3):
        network(rows_mem.at[i], w1, b1, w2, b2, w3, h1, h2, raw.at[i], beside[i])
    post(2)
    send(10, 12)
    for copy in outs:
        copy.wait()


def finish(p, u, v, left, right, tend, mid, weights, mask, courant, gain):
    shape = jax.ShapeDtypeStruct((WIDTH, LEVELS, ACROSS), F32)
    column = pltpu.VMEM((WIDTH, LEVELS, ACROSS), F32)
    return pl.pallas_call(
        finish_kernel,
        out_shape=(shape,) * 3,
        in_specs=[ANY] * 3 + [OPEN] * 2 + [ANY] * 7 + [VMEM] * 3,
        out_specs=(ANY,) * 3,
        scratch_shapes=[pltpu.VMEM((SPAN, LEVELS, ACROSS), F32)] + [column] * 3
        + [pltpu.VMEM((2, SENT, LEVELS, ACROSS), BF16)]
        + [pltpu.VMEM((WIDTH + 6, LEVELS, ACROSS), F32), column, column]
        + [pltpu.VMEM((7, LEVELS, ACROSS), F32)]
        + [pltpu.VMEM((WIDTH, 3, LEVELS, ACROSS), F32), pltpu.VMEM((3, LEVELS, 128), F32)]
        + [column] * 3
        + WEIGHTS_SCRATCH
        + [pltpu.SemaphoreType.DMA((17,))],
        compiler_params=pltpu.CompilerParams(vmem_limit_bytes=44 * 2**20),
        cost_estimate=pl.CostEstimate(
            flops=network_flops(WIDTH // 2 * ACROSS), bytes_accessed=12 * 2**20, transcendentals=0
        ),
        name="finish",
    )(p, u, v, left, right, tend, mid, *weights, mask, courant, gain)


def body(
    pressure, wind_x, wind_y, courant, send_list,
    norm_gain, w_first, b_first, w_second, b_second, w_last,
):
    p, u, v = [jnp.transpose(f, (1, 0, 2)) for f in (pressure, wind_x, wind_y)]
    courant, gain = courant.reshape(1, LEVELS), norm_gain.reshape(1, ROWS)
    lists = jnp.transpose(send_list, (2, 0, 1))
    weights = (w_first, b_first.reshape(1, UNITS), w_second, b_second.reshape(1, UNITS), w_last.T)
    to_next, to_prev = edges(p, u, v)
    left = lax.ppermute(to_next, AXES, [(i, (i + 1) % DEVICES) for i in range(DEVICES)])
    right = lax.ppermute(to_prev, AXES, [(i, (i - 1) % DEVICES) for i in range(DEVICES)])
    tend, mid, mask = interior(p, u, v, weights, courant, gain, lists)
    outs = finish(p, u, v, left, right, tend, mid, weights, mask, courant, gain)
    return tuple(jnp.transpose(f, (1, 0, 2)) for f in outs)


def solution(mesh):
    split = P(None, AXES, None)
    in_specs = (split,) * 3 + (P(), P(AXES, None, None)) + (P(),) * 6
    return jax.shard_map(
        body, mesh=mesh, in_specs=in_specs, out_specs=(split,) * 3, check_vma=False
    )
```

```python
import jax
import jax.numpy as jnp
from jax import lax
from jax.experimental import pallas as pl
from jax.experimental.pallas import tpu as pltpu
from jax.sharding import PartitionSpec as P

AXES = ("group", "tile")
LEVELS, WIDTH, ACROSS, UNITS, SLOTS, DEVICES = 60, 12, 384, 1024, 36, 128
ROWS = 3 * LEVELS
HALO = 6
SENT = 3 * HALO
OPEN = pl.BlockSpec(memory_space=pl.ANY)
SPAN = WIDTH + 2 * HALO
CHUNK = 2 * ACROSS
TILE = 256
F32, BF16 = jnp.float32, jnp.bfloat16
NN = (((1,), (0,)), ((), ()))
NT = (((1,), (1,)), ((), ()))
ANY = pl.BlockSpec(memory_space=pltpu.HBM)
VMEM = pl.BlockSpec(memory_space=pltpu.VMEM)


def lanes(shape):
    return lax.broadcasted_iota(jnp.int32, shape, len(shape) - 1)


def split(value):
    return [value[:, i : i + 128] for i in range(0, ACROSS, 128)]


def join(parts):
    return jnp.concatenate(parts, axis=1)


def run_copies(pairs, sems, first=0):
    copies = [
        pltpu.make_async_copy(src, dst, sems.at[first + i]) for i, (src, dst) in enumerate(pairs)
    ]
    for copy in copies:
        copy.start()
    return copies


def divergence(v):
    v = jnp.where(lanes(v.shape) < ACROSS - 1, v, 0.0)
    return v - pltpu.roll(v, 1, 1)


def rest(value):
    return (value - value.astype(BF16).astype(F32)).astype(BF16)


def edges_kernel(p_hbm, u_hbm, v_hbm, r_mem, l_mem, p_mem, u_mem, v_mem, sems):
    low, high = slice(0, HALO), slice(WIDTH - HALO, WIDTH)
    loads = run_copies(
        [(f.at[s], m.at[s]) for s in (high, low)
         for f, m in ((p_hbm, p_mem), (u_hbm, u_mem), (v_hbm, v_mem))],
        sems,
    )
    for copy in loads[:3]:
        copy.wait()
    for i in range(HALO):
        r_mem[i] = p_mem[WIDTH - HALO + i].astype(BF16)
    for i in range(HALO - 1):
        x = WIDTH - HALO + 1 + i
        div = (u_mem[x] - u_mem[x - 1]) + divergence(v_mem[x])
        r_mem[HALO + i] = div.astype(BF16)
        if x >= WIDTH - 2:
            r_mem[2 * HALO + 2 + WIDTH - x] = rest(div)
    r_mem[2 * HALO - 1] = u_mem[WIDTH - 1].astype(BF16)
    for i in range(3):
        r_mem[2 * HALO + i] = rest(p_mem[WIDTH - 1 - i])
    r_mem[SENT - 1] = rest(u_mem[WIDTH - 1])
    for copy in loads[3:]:
        copy.wait()
    for i in range(HALO):
        l_mem[i] = p_mem[i].astype(BF16)
    for x in range(HALO):
        west = u_mem[x - 1] if x else 0.0
        div = (u_mem[x] - west) + divergence(v_mem[x])
        l_mem[HALO + x] = div.astype(BF16)
        if x < 3:
            l_mem[2 * HALO + 3 + x] = rest(div)
    for i in range(3):
        l_mem[2 * HALO + i] = rest(p_mem[i])


def edges(p, u, v):
    shape = jax.ShapeDtypeStruct((SENT, LEVELS, ACROSS), BF16)
    return pl.pallas_call(
        edges_kernel,
        out_shape=(shape, shape),
        in_specs=[ANY] * 3,
        out_specs=(VMEM, VMEM),
        scratch_shapes=[pltpu.VMEM((WIDTH, LEVELS, ACROSS), F32)] * 3
        + [pltpu.SemaphoreType.DMA((6,))],
        compiler_params=pltpu.CompilerParams(vmem_limit_bytes=60 * 2**20),
        name="edges",
    )(p, u, v)


def stepping(count, low, high, square, load_p, load_d, done):
    ps = [{} for _ in range(count + 1)]
    ds = [{} for _ in range(count + 1)]
    sums = {}
    lane = lanes(square.shape)
    first, last = lane == 0, lane == 127

    def substep(k, x):
        west, here, east = (ps[k - 1][x + i] for i in (-1, 0, 1))
        down = [pltpu.roll(h, 127, 1) for h in here]
        up = [pltpu.roll(h, 1, 1) for h in here]
        north = [jnp.where(last, down[1], down[0]), jnp.where(last, down[2], down[1]),
                 jnp.where(last, here[2], down[2])]
        south = [jnp.where(first, here[0], up[0]), jnp.where(first, up[0], up[1]),
                 jnp.where(first, up[1], up[2])]
        ds[k][x] = [d - (((e + w) + (n + s)) - 4.0 * h)
                    for d, e, w, n, s, h in zip(ds[k - 1][x], east, west, north, south, here)]
        ps[k][x] = [h - square * d for h, d in zip(here, ds[k][x])]
        if k == count:
            done(x, ps[k][x], ds[k][x], sums[x], sums[x + 1])
        elif low + count - 1 <= x <= high - count + 1:
            sums[x] = [s + p for s, p in zip(sums[x], ps[k][x])]

    for t in range(low, high + 2 * count + 1):
        if t <= high:
            ps[0][t] = load_p(t)
            if low + count - 1 <= t <= high - count + 1:
                sums[t] = ps[0][t]
            if low < t < high:
                ds[0][t] = load_d(t)
        for k in range(1, count + 1):
            x = t - 2 * k
            if low + k <= x <= high - k:
                substep(k, x)
        yield


def march(*args):
    for _ in stepping(*args):
        pass


def march_both(one, two):
    for _ in zip(stepping(*one), stepping(*two), strict=True):
        pass


def own_divergence(u, west, v, inverse):
    lane = lanes(inverse.shape)
    first, last = lane == 0, lane == 127
    v = [v[0], v[1], jnp.where(last, 0.0, v[2])]
    up = [pltpu.roll(a, 1, 1) for a in v]
    south = [jnp.where(first, up[i - 1], up[i]) for i in range(3)]
    return [((a - w) + (b - s)) * inverse for a, w, b, s in zip(u, west, v, south)]


def winds(u, v, c, here, east):
    last = lanes(c.shape) == 127
    down = [pltpu.roll(s, 127, 1) for s in here]
    north = [jnp.where(last, down[1], down[0]), jnp.where(last, down[2], down[1]), down[2]]
    u = [a - c * (e - s) for a, e, s in zip(u, east, here)]
    v = [a - c * (n - s) for a, n, s in zip(v, north, here)]
    return u, [v[0], v[1], jnp.where(last, 0.0, v[2])]


def by_level(row):
    return jnp.broadcast_to(row, (128, row.shape[1])).T


def level_constants(courant_row, c_mem):
    c = by_level(courant_row)
    c_mem[0] = c
    c_mem[1] = c * c
    c_mem[2] = 1.0 / c


def group_rows(g):
    return pl.ds(8 * g, 8) if g < LEVELS // 8 else slice(LEVELS // 8 * 8, LEVELS)


def by_groups(work):
    def group(g, carry):
        work(pl.ds(pl.multiple_of(g * 8, 8), 8))
        return carry

    lax.fori_loop(0, LEVELS // 8, group, 0)
    work(group_rows(LEVELS // 8))


def silu(z):
    half = z * 0.5
    return half + half * jnp.tanh(half)


def normed_rows(read, gain, xs):
    columns = jnp.concatenate([jnp.concatenate(read(x), axis=0) for x in xs], axis=1)
    values = columns.astype(BF16).astype(F32)
    mean = jnp.sum(values * values, axis=0, keepdims=True) * (1.0 / ROWS)
    return (values * lax.rsqrt(mean + 1e-05) * gain).astype(BF16).T


def network(rows, w1, b1, w2, b2, w3, h1, h2, raw, beside=()):
    for n in range(0, UNITS, TILE):
        z = lax.dot_general(rows[...], w1[:, n : n + TILE], NN, preferred_element_type=F32)
        h1[:, n : n + TILE] = silu(z + b1[:, n : n + TILE]).astype(BF16)
    for n in range(0, UNITS, TILE):
        z = lax.dot_general(h1[...], w2[:, n : n + TILE], NN, preferred_element_type=F32)
        h2[:, n : n + TILE] = silu(z + b2[:, n : n + TILE]).astype(BF16)
        if n // TILE < len(beside):
            beside[n // TILE]()
    raw[...] = lax.dot_general(h2[...], w3[...], NN, preferred_element_type=F32)


def store_tendency(raw, mask, xs, places, out):
    t = raw[...].T.astype(BF16).astype(F32)
    for i, (x, place) in enumerate(zip(xs, places)):
        row = jnp.concatenate([mask[3 * x + j : 3 * x + j + 1, :] for j in range(3)], axis=1)
        listed = jnp.where(row > 0.5, t[:, i * ACROSS : (i + 1) * ACROSS], 0.0)
        for f in range(3):
            out[place, f] = listed[f * LEVELS : (f + 1) * LEVELS]


WEIGHTS_SCRATCH = [
    pltpu.VMEM((ROWS, UNITS), BF16),
    pltpu.VMEM((1, UNITS), F32),
    pltpu.VMEM((UNITS, UNITS), BF16),
    pltpu.VMEM((1, UNITS), F32),
    pltpu.VMEM((ROWS, UNITS), BF16),
    pltpu.VMEM((UNITS, ROWS), BF16),
    pltpu.VMEM((CHUNK, UNITS), BF16),
    pltpu.VMEM((CHUNK, UNITS), BF16),
    pltpu.VMEM((3, CHUNK, ROWS), BF16),
    pltpu.VMEM((3, CHUNK, ROWS), F32),
]


def network_flops(columns):
    return 2 * columns * (2 * ROWS * UNITS + UNITS * UNITS)


def interior_kernel(
    p_hbm, u_hbm, v_hbm, w1_hbm, b1_hbm, w2_hbm, b2_hbm, w3_hbm, courant, gain, lists,
    tend, mid, mask,
    p_mem, u_mem, v_mem, m_mem, t_mem, c_mem, one_x, one_y,
    w1, b1, w2, b2, w3t, w3, h1, h2, rows_mem, raw, sems,
):
    near, far = slice(0, 8), slice(8, WIDTH)
    fields = run_copies(
        [(f.at[s], m.at[s]) for s in (near, far)
         for f, m in ((p_hbm, p_mem), (u_hbm, u_mem), (v_hbm, v_mem))],
        sems,
    )
    weights = run_copies([(w3_hbm, w3t), (w1_hbm, w1), (b1_hbm, b1), (w2_hbm, w2), (b2_hbm, b2)],
                         sems, 6)
    level_constants(courant[...], c_mem)
    gain_column = by_level(gain[...])[:, :1]
    for s in range(SLOTS):
        entry = lists[s]
        part, spot = entry >> 7, entry & 127
        where = slice(s * DEVICES, (s + 1) * DEVICES)
        one_x[:, where] = (
            lax.broadcasted_iota(jnp.int32, (48, DEVICES), 0) == part
        ).astype(F32).astype(BF16)
        one_y[:, where] = (
            lax.broadcasted_iota(jnp.int32, (128, DEVICES), 0) == spot
        ).astype(F32).astype(BF16)
    mask[...] = lax.dot_general(one_x[...], one_y[...], NT, preferred_element_type=F32)

    def columns(rows, *pairs):
        c, square, inverse = (c_mem[j, rows, :] for j in range(3))

        def done(x, p, d, here, east):
            u, v = winds(split(u_mem[x, rows, :]), split(v_mem[x, rows, :]), c, here, east)
            for f, value in enumerate((p, u, v)):
                m_mem[f, x - 3, rows, :] = join(value)

        def load_d(x):
            return own_divergence(split(u_mem[x, rows, :]), split(u_mem[x - 1, rows, :]),
                                  split(v_mem[x, rows, :]), inverse)

        return [(3, 2 * i, 2 * i + 7, square, lambda x: split(p_mem[x, rows, :]), load_d, done)
                for i in pairs]

    def first_pair(rows, more):
        march_both(*columns(rows, 0), *columns(more, 0))

    def two_groups(g, carry):
        at = pl.multiple_of(g * 16, 16)
        first_pair(pl.ds(at, 8), pl.ds(pl.multiple_of(at + 8, 8), 8))
        return carry

    def other_pairs(low, high):
        def run():
            for g in range(low, high):
                march_both(*columns(group_rows(g), 1, 2))
        return run

    def read(x):
        return [m_mem[f, x] for f in range(3)]

    def prepare(i):
        rows_mem[i] = normed_rows(read, gain_column, (2 * i, 2 * i + 1))

    sent = []

    def post(i):
        xs = (2 * i, 2 * i + 1)
        store_tendency(raw.at[i], mask, [x + 3 for x in xs], xs, t_mem)
        sent.extend(run_copies([(t_mem.at[2 * i : 2 * i + 2], tend.at[2 * i : 2 * i + 2])],
                               sems, 11 + i))

    def both(*works):
        def run():
            for work in works:
                work()
        return run

    for copy in fields[:3]:
        copy.wait()
    lax.fori_loop(0, LEVELS // 16, two_groups, 0)
    first_pair(group_rows(6), group_rows(7))
    for copy in fields[3:]:
        copy.wait()
    prepare(0)
    for copy in weights:
        copy.wait()
    w3[...] = w3t[...].T
    beside = (
        [other_pairs(0, 2), other_pairs(2, 4), other_pairs(4, 6),
         both(other_pairs(6, 8), lambda: prepare(1))],
        [lambda: post(0), lambda: prepare(2)],
        [lambda: sent.extend(run_copies([(m_mem, mid)], sems, 14)), lambda: post(1)],
    )
    for i in range(3):
        network(rows_mem.at[i], w1, b1, w2, b2, w3, h1, h2, raw.at[i], beside[i])
    post(2)
    for copy in sent:
        copy.wait()


def interior(p, u, v, weights, courant, gain, lists):
    column = pltpu.VMEM((WIDTH, LEVELS, ACROSS), F32)
    return pl.pallas_call(
        interior_kernel,
        out_shape=(
            jax.ShapeDtypeStruct((WIDTH // 2, 3, LEVELS, ACROSS), F32),
            jax.ShapeDtypeStruct((3, WIDTH // 2, LEVELS, ACROSS), F32),
            jax.ShapeDtypeStruct((48, 128), F32),
        ),
        in_specs=[ANY] * 8 + [VMEM] * 3,
        out_specs=(ANY, ANY, VMEM),
        scratch_shapes=[column] * 3
        + [pltpu.VMEM((3, WIDTH // 2, LEVELS, ACROSS), F32)]
        + [pltpu.VMEM((WIDTH // 2, 3, LEVELS, ACROSS), F32), pltpu.VMEM((3, LEVELS, 128), F32)]
        + [pltpu.VMEM((48, SLOTS * DEVICES), BF16), pltpu.VMEM((128, SLOTS * DEVICES), BF16)]
        + WEIGHTS_SCRATCH
        + [pltpu.SemaphoreType.DMA((15,))],
        compiler_params=pltpu.CompilerParams(vmem_limit_bytes=52 * 2**20),
        cost_estimate=pl.CostEstimate(
            flops=network_flops(WIDTH // 2 * ACROSS), bytes_accessed=8 * 2**20, transcendentals=0
        ),
        name="interior",
    )(p, u, v, *weights, courant, gain, lists)


def finish_kernel(
    p_hbm, u_hbm, v_hbm, left, right, tend, mid, w1_hbm, b1_hbm, w2_hbm, b2_hbm, w3_hbm,
    mask, courant, gain,
    p_out, u_out, v_out,
    p_mem, u_mem, v_mem, e_mem, halo, a_mem, b_mem, d_mem, g_mem, t_mem, c_mem,
    p_new, u_new, v_new,
    w1, b1, w2, b2, w3t, w3, h1, h2, rows_mem, raw, sems,
):
    near, far = slice(0, HALO), slice(HALO, WIDTH)
    fields = run_copies(
        [
            (left, halo.at[0]),
            (p_hbm.at[near], p_mem.at[HALO : 2 * HALO]),
            (u_hbm.at[near], u_mem.at[near]),
            (v_hbm.at[near], v_mem.at[near]),
            (right, halo.at[1]),
            (p_hbm.at[far], p_mem.at[2 * HALO : 3 * HALO]),
            (u_hbm.at[far], u_mem.at[far]),
            (v_hbm.at[far], v_mem.at[far]),
        ],
        sems,
    )

    def start_weights():
        return run_copies(
            [(w3_hbm, w3t), (w1_hbm, w1), (b1_hbm, b1), (w2_hbm, w2), (b2_hbm, b2),
             (mid.at[0], a_mem.at[6:12]), (mid.at[1], b_mem.at[3:9]), (mid.at[2], d_mem.at[3:9]),
             (tend, t_mem.at[3:9])],
            sems, 8,
        )

    level_constants(courant[...], c_mem)
    gain_column = by_level(gain[...])[:, :1]

    def loads(rows, inverse):
        def load_p(x):
            return split(p_mem[x + HALO, rows, :])

        def load_d(x):
            if x < 0:
                return [d * inverse for d in split(e_mem[x + HALO - 1, rows, :])]
            if x > WIDTH:
                return [d * inverse for d in split(e_mem[x - HALO, rows, :])]
            if x == WIDTH:
                return [(d - u) * inverse for d, u in zip(split(e_mem[HALO, rows, :]),
                                                          split(u_mem[WIDTH - 1, rows, :]))]
            west = u_mem[x - 1, rows, :] if x else e_mem[HALO - 1, rows, :]
            return own_divergence(split(u_mem[x, rows, :]), split(west),
                                  split(v_mem[x, rows, :]), inverse)

        return load_p, load_d

    def strips(rows):
        c, square, inverse = (c_mem[i, rows, :] for i in range(3))

        def done(x, p, d, here, east):
            a_mem[x + 3, rows, :] = join(p)
            u, v = winds(split(u_mem[x, rows, :]), split(v_mem[x, rows, :]), c, here, east)
            b_mem[x, rows, :] = join(u)
            d_mem[x, rows, :] = join(v)
            if x == 0:
                g_mem[3, rows, :] = join(d)

        common = (square, *loads(rows, inverse), done)
        march_both((3, -3, 5, *common), (3, 6, 14, *common))

    for copy in fields[:4]:
        copy.wait()
    for i in range(HALO):
        p_mem[i] = halo[0, i].astype(F32)
        e_mem[i] = halo[0, HALO + i].astype(F32)
    for i, (near_p, near_e) in enumerate(((1, 2), (2, 3), (3, 1))):
        p_mem[HALO - near_p] = p_mem[HALO - near_p] + halo[0, 2 * HALO + i].astype(F32)
        e_mem[HALO - near_e] = e_mem[HALO - near_e] + halo[0, 2 * HALO + 3 + i].astype(F32)
    for copy in fields[4:]:
        copy.wait()
    for i in range(HALO):
        p_mem[HALO + WIDTH + i] = halo[1, i].astype(F32)
        e_mem[HALO + i] = halo[1, HALO + i].astype(F32)
    for i in range(3):
        p_mem[HALO + WIDTH + i] = p_mem[HALO + WIDTH + i] + halo[1, 2 * HALO + i].astype(F32)
        e_mem[HALO + i] = e_mem[HALO + i] + halo[1, 2 * HALO + 3 + i].astype(F32)
    weights = start_weights()
    by_groups(strips)

    def dynamics(g):
        rows = group_rows(g)
        c, square, inverse = (c_mem[i, rows, :] for i in range(3))

        def outer(x, p, d, here, east):
            a_mem[x + 3, rows, :] = join(p)
            g_mem[x + 3 if x < 0 else x - 8, rows, :] = join(d)

        common = (square, *loads(rows, inverse), outer)
        march_both((3, -6, 2, *common), (3, 9, 17, *common))

        def load_d(x):
            if 0 < x < WIDTH:
                return own_divergence(split(b_mem[x, rows, :]), split(b_mem[x - 1, rows, :]),
                                      split(d_mem[x, rows, :]), inverse)
            return split(g_mem[x + 3 if x <= 0 else x - 8, rows, :])

        def done(x, p, d, here, east):
            p_new[x, rows, :] = join(p)
            u, v = winds(split(b_mem[x, rows, :]), split(d_mem[x, rows, :]), c, here, east)
            u_new[x, rows, :] = join(u)
            v_new[x, rows, :] = join(v)

        march(3, -3, 14, square, lambda x: split(a_mem[x + 3, rows, :]), load_d, done)

    columns = (0, 1, 2, 9, 10, 11)

    def read(x):
        return a_mem[x + 3], b_mem[x], d_mem[x]

    def prepare(i):
        rows_mem[i] = normed_rows(read, gain_column, columns[2 * i : 2 * i + 2])

    def post(i):
        xs = columns[2 * i : 2 * i + 2]
        store_tendency(raw.at[i], mask, xs, xs, t_mem)

    outs = []

    def send(low, high):
        for x in range(low, high):
            for f, new in enumerate((p_new, u_new, v_new)):
                new[x] = new[x] + t_mem[x, f]
        outs.extend(run_copies(
            [(new.at[low:high], out.at[low:high])
             for new, out in ((p_new, p_out), (u_new, u_out), (v_new, v_out))],
            sems, len(outs),
        ))

    def both(*works):
        def run():
            for work in works:
                work()
        return run

    def group(g):
        return lambda: dynamics(g)

    prepare(0)
    for copy in weights:
        copy.wait()
    w3[...] = w3t[...].T
    beside = (
        [group(0), group(1), group(2), lambda: prepare(1)],
        [group(3), group(4), group(5), both(lambda: prepare(2), lambda: post(0))],
        [group(6), group(7), both(lambda: post(1), lambda: send(0, 4)), lambda: send(4, 10)],
    )
    for i in range(3):
        network(rows_mem.at[i], w1, b1, w2, b2, w3, h1, h2, raw.at[i], beside[i])
    post(2)
    send(10, 12)
    for copy in outs:
        copy.wait()


def finish(p, u, v, left, right, tend, mid, weights, mask, courant, gain):
    shape = jax.ShapeDtypeStruct((WIDTH, LEVELS, ACROSS), F32)
    column = pltpu.VMEM((WIDTH, LEVELS, ACROSS), F32)
    return pl.pallas_call(
        finish_kernel,
        out_shape=(shape,) * 3,
        in_specs=[ANY] * 3 + [OPEN] * 2 + [ANY] * 7 + [VMEM] * 3,
        out_specs=(ANY,) * 3,
        scratch_shapes=[pltpu.VMEM((SPAN, LEVELS, ACROSS), F32)] + [column] * 3
        + [pltpu.VMEM((2, SENT, LEVELS, ACROSS), BF16)]
        + [pltpu.VMEM((WIDTH + 6, LEVELS, ACROSS), F32), column, column]
        + [pltpu.VMEM((7, LEVELS, ACROSS), F32)]
        + [pltpu.VMEM((WIDTH, 3, LEVELS, ACROSS), F32), pltpu.VMEM((3, LEVELS, 128), F32)]
        + [column] * 3
        + WEIGHTS_SCRATCH
        + [pltpu.SemaphoreType.DMA((17,))],
        compiler_params=pltpu.CompilerParams(vmem_limit_bytes=48 * 2**20),
        cost_estimate=pl.CostEstimate(
            flops=network_flops(WIDTH // 2 * ACROSS), bytes_accessed=12 * 2**20, transcendentals=0
        ),
        name="finish",
    )(p, u, v, left, right, tend, mid, *weights, mask, courant, gain)


def body(
    pressure, wind_x, wind_y, courant, send_list,
    norm_gain, w_first, b_first, w_second, b_second, w_last,
):
    p, u, v = [jnp.transpose(f, (1, 0, 2)) for f in (pressure, wind_x, wind_y)]
    courant, gain = courant.reshape(1, LEVELS), norm_gain.reshape(1, ROWS)
    lists = jnp.transpose(send_list, (2, 0, 1))
    weights = (w_first, b_first.reshape(1, UNITS), w_second, b_second.reshape(1, UNITS), w_last.T)
    to_next, to_prev = edges(p, u, v)
    left = lax.ppermute(to_next, AXES, [(i, (i + 1) % DEVICES) for i in range(DEVICES)])
    right = lax.ppermute(to_prev, AXES, [(i, (i - 1) % DEVICES) for i in range(DEVICES)])
    tend, mid, mask = interior(p, u, v, weights, courant, gain, lists)
    outs = finish(p, u, v, left, right, tend, mid, weights, mask, courant, gain)
    return tuple(jnp.transpose(f, (1, 0, 2)) for f in outs)


def solution(mesh):
    split = P(None, AXES, None)
    in_specs = (split,) * 3 + (P(), P(AXES, None, None)) + (P(),) * 6
    return jax.shard_map(
        body, mesh=mesh, in_specs=in_specs, out_specs=(split,) * 3, check_vma=False
    )
```

```python
import jax
import jax.numpy as jnp
from jax import lax
from jax.experimental import pallas as pl
from jax.experimental.pallas import tpu as pltpu
from jax.sharding import PartitionSpec as P

AXES = ("group", "tile")
LEVELS, WIDTH, ACROSS, UNITS, SLOTS, DEVICES = 60, 12, 384, 1024, 36, 128
ROWS = 3 * LEVELS
HALO = 6
SENT = 3 * HALO
CHUNK = 2 * ACROSS
TILE = 256
F32, BF16 = jnp.float32, jnp.bfloat16
NN = (((1,), (0,)), ((), ()))
NT = (((1,), (1,)), ((), ()))
ANY = pl.BlockSpec(memory_space=pltpu.HBM)
VMEM = pl.BlockSpec(memory_space=pltpu.VMEM)


def lanes(shape):
    return lax.broadcasted_iota(jnp.int32, shape, len(shape) - 1)


def split(value):
    return [value[:, i : i + 128] for i in range(0, ACROSS, 128)]


def join(parts):
    return jnp.concatenate(parts, axis=1)


def run_copies(pairs, sems, first=0):
    copies = [
        pltpu.make_async_copy(src, dst, sems.at[first + i]) for i, (src, dst) in enumerate(pairs)
    ]
    for copy in copies:
        copy.start()
    return copies


def divergence(v):
    v = jnp.where(lanes(v.shape) < ACROSS - 1, v, 0.0)
    return v - pltpu.roll(v, 1, 1)


def rest(value):
    return (value - value.astype(BF16).astype(F32)).astype(BF16)


def edges_kernel(p_hbm, u_hbm, v_hbm, r_mem, l_mem, p_mem, u_mem, v_mem, sems):
    low, high = slice(0, HALO), slice(WIDTH - HALO, WIDTH)
    loads = run_copies(
        [(f.at[s], m.at[s]) for s in (high, low)
         for f, m in ((p_hbm, p_mem), (u_hbm, u_mem), (v_hbm, v_mem))],
        sems,
    )
    for copy in loads[:3]:
        copy.wait()
    for i in range(HALO):
        r_mem[i] = p_mem[WIDTH - HALO + i].astype(BF16)
    for i in range(HALO - 1):
        x = WIDTH - HALO + 1 + i
        div = (u_mem[x] - u_mem[x - 1]) + divergence(v_mem[x])
        r_mem[HALO + i] = div.astype(BF16)
        if x >= WIDTH - 2:
            r_mem[2 * HALO + 2 + WIDTH - x] = rest(div)
    r_mem[2 * HALO - 1] = u_mem[WIDTH - 1].astype(BF16)
    for i in range(3):
        r_mem[2 * HALO + i] = rest(p_mem[WIDTH - 1 - i])
    r_mem[SENT - 1] = rest(u_mem[WIDTH - 1])
    for copy in loads[3:]:
        copy.wait()
    for i in range(HALO):
        l_mem[i] = p_mem[i].astype(BF16)
    for x in range(HALO):
        west = u_mem[x - 1] if x else 0.0
        div = (u_mem[x] - west) + divergence(v_mem[x])
        l_mem[HALO + x] = div.astype(BF16)
        if x < 3:
            l_mem[2 * HALO + 3 + x] = rest(div)
    for i in range(3):
        l_mem[2 * HALO + i] = rest(p_mem[i])


def edges(p, u, v):
    shape = jax.ShapeDtypeStruct((SENT, LEVELS, ACROSS), BF16)
    return pl.pallas_call(
        edges_kernel,
        out_shape=(shape, shape),
        in_specs=[ANY] * 3,
        out_specs=(VMEM, VMEM),
        scratch_shapes=[pltpu.VMEM((WIDTH, LEVELS, ACROSS), F32)] * 3
        + [pltpu.SemaphoreType.DMA((6,))],
        compiler_params=pltpu.CompilerParams(vmem_limit_bytes=60 * 2**20),
        name="edges",
    )(p, u, v)


def stepping(count, low, high, square, load_p, load_d, done):
    ps = [{} for _ in range(count + 1)]
    ds = [{} for _ in range(count + 1)]
    sums = {}
    lane = lanes(square.shape)
    first, last = lane == 0, lane == 127

    def substep(k, x):
        west, here, east = (ps[k - 1][x + i] for i in (-1, 0, 1))
        down = [pltpu.roll(h, 127, 1) for h in here]
        up = [pltpu.roll(h, 1, 1) for h in here]
        north = [jnp.where(last, down[1], down[0]), jnp.where(last, down[2], down[1]),
                 jnp.where(last, here[2], down[2])]
        south = [jnp.where(first, here[0], up[0]), jnp.where(first, up[0], up[1]),
                 jnp.where(first, up[1], up[2])]
        ds[k][x] = [d - (((e + w) + (n + s)) - 4.0 * h)
                    for d, e, w, n, s, h in zip(ds[k - 1][x], east, west, north, south, here)]
        ps[k][x] = [h - square * d for h, d in zip(here, ds[k][x])]
        if k == count:
            done(x, ps[k][x], ds[k][x], sums[x], sums[x + 1])
        elif low + count - 1 <= x <= high - count + 1:
            sums[x] = [s + p for s, p in zip(sums[x], ps[k][x])]

    for t in range(low, high + 2 * count + 1):
        if t <= high:
            ps[0][t] = load_p(t)
            if low + count - 1 <= t <= high - count + 1:
                sums[t] = ps[0][t]
            if low < t < high:
                ds[0][t] = load_d(t)
        for k in range(1, count + 1):
            x = t - 2 * k
            if low + k <= x <= high - k:
                substep(k, x)
        yield


def march(*args):
    for _ in stepping(*args):
        pass


def march_both(one, two):
    for _ in zip(stepping(*one), stepping(*two), strict=True):
        pass


def own_divergence(u, west, v, inverse):
    lane = lanes(inverse.shape)
    first, last = lane == 0, lane == 127
    v = [v[0], v[1], jnp.where(last, 0.0, v[2])]
    up = [pltpu.roll(a, 1, 1) for a in v]
    south = [jnp.where(first, up[i - 1], up[i]) for i in range(3)]
    return [((a - w) + (b - s)) * inverse for a, w, b, s in zip(u, west, v, south)]


def winds(u, v, c, here, east):
    last = lanes(c.shape) == 127
    down = [pltpu.roll(s, 127, 1) for s in here]
    north = [jnp.where(last, down[1], down[0]), jnp.where(last, down[2], down[1]), down[2]]
    u = [a - c * (e - s) for a, e, s in zip(u, east, here)]
    v = [a - c * (n - s) for a, n, s in zip(v, north, here)]
    return u, [v[0], v[1], jnp.where(last, 0.0, v[2])]


def by_level(row):
    return jnp.broadcast_to(row, (128, row.shape[1])).T


def level_constants(courant_row, c_mem):
    c = by_level(courant_row)
    c_mem[0] = c
    c_mem[1] = c * c
    c_mem[2] = 1.0 / c


def group_rows(g):
    return pl.ds(8 * g, 8) if g < LEVELS // 8 else slice(LEVELS // 8 * 8, LEVELS)


def by_groups(work):
    def group(g, carry):
        work(pl.ds(pl.multiple_of(g * 8, 8), 8))
        return carry

    lax.fori_loop(0, LEVELS // 8, group, 0)
    work(group_rows(LEVELS // 8))


def silu(z):
    half = z * 0.5
    return half + half * jnp.tanh(half)


def normed_rows(read, gain, xs):
    columns = jnp.concatenate([jnp.concatenate(read(x), axis=0) for x in xs], axis=1)
    values = columns.astype(BF16).astype(F32)
    mean = jnp.sum(values * values, axis=0, keepdims=True) * (1.0 / ROWS)
    return (values * lax.rsqrt(mean + 1e-05) * gain).astype(BF16).T


def network(rows, w1, b1, w2, b2, w3, h1, h2, raw, beside=()):
    for n in range(0, UNITS, TILE):
        z = lax.dot_general(rows[...], w1[:, n : n + TILE], NN, preferred_element_type=F32)
        h1[:, n : n + TILE] = silu(z + b1[:, n : n + TILE]).astype(BF16)
    for n in range(0, UNITS, TILE):
        z = lax.dot_general(h1[...], w2[:, n : n + TILE], NN, preferred_element_type=F32)
        h2[:, n : n + TILE] = silu(z + b2[:, n : n + TILE]).astype(BF16)
        if n // TILE < len(beside):
            beside[n // TILE]()
    raw[...] = lax.dot_general(h2[...], w3[...], NN, preferred_element_type=F32)


def store_tendency(raw, mask, xs, places, out):
    t = raw[...].T.astype(BF16).astype(F32)
    for i, (x, place) in enumerate(zip(xs, places)):
        row = jnp.concatenate([mask[3 * x + j : 3 * x + j + 1, :] for j in range(3)], axis=1)
        listed = jnp.where(row > 0.5, t[:, i * ACROSS : (i + 1) * ACROSS], 0.0)
        for f in range(3):
            out[place, f] = listed[f * LEVELS : (f + 1) * LEVELS]


WEIGHTS_SCRATCH = [
    pltpu.VMEM((ROWS, UNITS), BF16),
    pltpu.VMEM((1, UNITS), F32),
    pltpu.VMEM((UNITS, UNITS), BF16),
    pltpu.VMEM((1, UNITS), F32),
    pltpu.VMEM((ROWS, UNITS), BF16),
    pltpu.VMEM((UNITS, ROWS), BF16),
    pltpu.VMEM((CHUNK, UNITS), BF16),
    pltpu.VMEM((CHUNK, UNITS), BF16),
    pltpu.VMEM((3, CHUNK, ROWS), BF16),
    pltpu.VMEM((3, CHUNK, ROWS), F32),
]


def network_flops(columns):
    return 2 * columns * (2 * ROWS * UNITS + UNITS * UNITS)


def interior_kernel(
    p_hbm, u_hbm, v_hbm, w1_hbm, b1_hbm, w2_hbm, b2_hbm, w3_hbm, courant, gain, lists,
    tend, mid, mask,
    p_mem, u_mem, v_mem, m_mem, t_mem, c_mem, one_x, one_y,
    w1, b1, w2, b2, w3t, w3, h1, h2, rows_mem, raw, sems,
):
    near, far = slice(0, 8), slice(8, WIDTH)
    fields = run_copies(
        [(f.at[s], m.at[s]) for s in (near, far)
         for f, m in ((p_hbm, p_mem), (u_hbm, u_mem), (v_hbm, v_mem))],
        sems,
    )
    weights = run_copies([(w3_hbm, w3t), (w1_hbm, w1), (b1_hbm, b1), (w2_hbm, w2), (b2_hbm, b2)],
                         sems, 6)
    level_constants(courant[...], c_mem)
    gain_column = by_level(gain[...])[:, :1]
    for s in range(SLOTS):
        entry = lists[s]
        part, spot = entry >> 7, entry & 127
        where = slice(s * DEVICES, (s + 1) * DEVICES)
        one_x[:, where] = (
            lax.broadcasted_iota(jnp.int32, (48, DEVICES), 0) == part
        ).astype(F32).astype(BF16)
        one_y[:, where] = (
            lax.broadcasted_iota(jnp.int32, (128, DEVICES), 0) == spot
        ).astype(F32).astype(BF16)
    mask[...] = lax.dot_general(one_x[...], one_y[...], NT, preferred_element_type=F32)

    def columns(rows, *pairs):
        c, square, inverse = (c_mem[j, rows, :] for j in range(3))

        def done(x, p, d, here, east):
            u, v = winds(split(u_mem[x, rows, :]), split(v_mem[x, rows, :]), c, here, east)
            for f, value in enumerate((p, u, v)):
                m_mem[f, x - 3, rows, :] = join(value)

        def load_d(x):
            return own_divergence(split(u_mem[x, rows, :]), split(u_mem[x - 1, rows, :]),
                                  split(v_mem[x, rows, :]), inverse)

        return [(3, 2 * i, 2 * i + 7, square, lambda x: split(p_mem[x, rows, :]), load_d, done)
                for i in pairs]

    def first_pair(rows, more):
        march_both(*columns(rows, 0), *columns(more, 0))

    def two_groups(g, carry):
        at = pl.multiple_of(g * 16, 16)
        first_pair(pl.ds(at, 8), pl.ds(pl.multiple_of(at + 8, 8), 8))
        return carry

    def other_pairs(low, high):
        def run():
            for g in range(low, high):
                march_both(*columns(group_rows(g), 1, 2))
        return run

    def read(x):
        return [m_mem[f, x] for f in range(3)]

    def prepare(i):
        rows_mem[i] = normed_rows(read, gain_column, (2 * i, 2 * i + 1))

    sent = []

    def post(i):
        xs = (2 * i, 2 * i + 1)
        store_tendency(raw.at[i], mask, [x + 3 for x in xs], xs, t_mem)
        sent.extend(run_copies([(t_mem.at[2 * i : 2 * i + 2], tend.at[2 * i : 2 * i + 2])],
                               sems, 11 + i))

    def both(*works):
        def run():
            for work in works:
                work()
        return run

    for copy in fields[:3]:
        copy.wait()
    lax.fori_loop(0, LEVELS // 16, two_groups, 0)
    first_pair(group_rows(6), group_rows(7))
    for copy in fields[3:]:
        copy.wait()
    prepare(0)
    for copy in weights:
        copy.wait()
    w3[...] = w3t[...].T
    beside = (
        [other_pairs(0, 2), other_pairs(2, 4), other_pairs(4, 6),
         both(other_pairs(6, 8), lambda: prepare(1))],
        [lambda: post(0), lambda: prepare(2)],
        [lambda: sent.extend(run_copies([(m_mem, mid)], sems, 14)), lambda: post(1)],
    )
    for i in range(3):
        network(rows_mem.at[i], w1, b1, w2, b2, w3, h1, h2, raw.at[i], beside[i])
    post(2)
    for copy in sent:
        copy.wait()


def interior(p, u, v, weights, courant, gain, lists):
    column = pltpu.VMEM((WIDTH, LEVELS, ACROSS), F32)
    return pl.pallas_call(
        interior_kernel,
        out_shape=(
            jax.ShapeDtypeStruct((WIDTH // 2, 3, LEVELS, ACROSS), F32),
            jax.ShapeDtypeStruct((3, WIDTH // 2, LEVELS, ACROSS), F32),
            jax.ShapeDtypeStruct((48, 128), F32),
        ),
        in_specs=[ANY] * 8 + [VMEM] * 3,
        out_specs=(ANY, ANY, VMEM),
        scratch_shapes=[column] * 3
        + [pltpu.VMEM((3, WIDTH // 2, LEVELS, ACROSS), F32)]
        + [pltpu.VMEM((WIDTH // 2, 3, LEVELS, ACROSS), F32), pltpu.VMEM((3, LEVELS, 128), F32)]
        + [pltpu.VMEM((48, SLOTS * DEVICES), BF16), pltpu.VMEM((128, SLOTS * DEVICES), BF16)]
        + WEIGHTS_SCRATCH
        + [pltpu.SemaphoreType.DMA((15,))],
        compiler_params=pltpu.CompilerParams(vmem_limit_bytes=52 * 2**20),
        cost_estimate=pl.CostEstimate(
            flops=network_flops(WIDTH // 2 * ACROSS), bytes_accessed=8 * 2**20, transcendentals=0
        ),
        name="interior",
    )(p, u, v, *weights, courant, gain, lists)


def finish_kernel(
    p_own, u_mem, v_mem, left, right, tend, mid, w1_hbm, b1_hbm, w2_hbm, b2_hbm, w3_hbm,
    mask, courant, gain,
    p_out, u_out, v_out,
    p_mem, e_mem, a_mem, b_mem, d_mem, g_mem, t_mem, c_mem,
    p_new, u_new, v_new,
    w1, b1, w2, b2, w3t, w3, h1, h2, rows_mem, raw, sems,
):
    weights = run_copies(
        [(w3_hbm, w3t), (w1_hbm, w1), (b1_hbm, b1), (w2_hbm, w2), (b2_hbm, b2),
         (mid.at[0], a_mem.at[6:12]), (mid.at[1], b_mem.at[3:9]), (mid.at[2], d_mem.at[3:9]),
         (tend, t_mem.at[3:9])],
        sems, 8,
    )
    level_constants(courant[...], c_mem)
    gain_column = by_level(gain[...])[:, :1]

    def loads(rows, inverse):
        def load_p(x):
            if 0 <= x < WIDTH:
                return split(p_own[x, rows, :])
            return split(p_mem[x + HALO if x < 0 else x - HALO, rows, :])

        def load_d(x):
            if x < 0:
                return [d * inverse for d in split(e_mem[x + HALO - 1, rows, :])]
            if x > WIDTH:
                return [d * inverse for d in split(e_mem[x - HALO, rows, :])]
            if x == WIDTH:
                return [(d - u) * inverse for d, u in zip(split(e_mem[HALO, rows, :]),
                                                          split(u_mem[WIDTH - 1, rows, :]))]
            west = u_mem[x - 1, rows, :] if x else e_mem[HALO - 1, rows, :]
            return own_divergence(split(u_mem[x, rows, :]), split(west),
                                  split(v_mem[x, rows, :]), inverse)

        return load_p, load_d

    def strips(rows):
        c, square, inverse = (c_mem[i, rows, :] for i in range(3))

        def done(x, p, d, here, east):
            a_mem[x + 3, rows, :] = join(p)
            u, v = winds(split(u_mem[x, rows, :]), split(v_mem[x, rows, :]), c, here, east)
            b_mem[x, rows, :] = join(u)
            d_mem[x, rows, :] = join(v)
            if x == 0:
                g_mem[3, rows, :] = join(d)

        common = (square, *loads(rows, inverse), done)
        march_both((3, -3, 5, *common), (3, 6, 14, *common))

    for i in range(HALO):
        p_mem[i] = left[i].astype(F32)
        e_mem[i] = left[HALO + i].astype(F32)
        p_mem[HALO + i] = right[i].astype(F32)
        e_mem[HALO + i] = right[HALO + i].astype(F32)
    for i, (near_p, near_e) in enumerate(((1, 2), (2, 3), (3, 1))):
        p_mem[HALO - near_p] = p_mem[HALO - near_p] + left[2 * HALO + i].astype(F32)
        e_mem[HALO - near_e] = e_mem[HALO - near_e] + left[2 * HALO + 3 + i].astype(F32)
        p_mem[HALO + i] = p_mem[HALO + i] + right[2 * HALO + i].astype(F32)
        e_mem[HALO + i] = e_mem[HALO + i] + right[2 * HALO + 3 + i].astype(F32)
    by_groups(strips)

    def dynamics(g):
        rows = group_rows(g)
        c, square, inverse = (c_mem[i, rows, :] for i in range(3))

        def outer(x, p, d, here, east):
            a_mem[x + 3, rows, :] = join(p)
            g_mem[x + 3 if x < 0 else x - 8, rows, :] = join(d)

        common = (square, *loads(rows, inverse), outer)
        march_both((3, -6, 2, *common), (3, 9, 17, *common))

        def load_d(x):
            if 0 < x < WIDTH:
                return own_divergence(split(b_mem[x, rows, :]), split(b_mem[x - 1, rows, :]),
                                      split(d_mem[x, rows, :]), inverse)
            return split(g_mem[x + 3 if x <= 0 else x - 8, rows, :])

        def done(x, p, d, here, east):
            p_new[x, rows, :] = join(p)
            u, v = winds(split(b_mem[x, rows, :]), split(d_mem[x, rows, :]), c, here, east)
            u_new[x, rows, :] = join(u)
            v_new[x, rows, :] = join(v)

        march(3, -3, 14, square, lambda x: split(a_mem[x + 3, rows, :]), load_d, done)

    columns = (0, 1, 2, 9, 10, 11)

    def read(x):
        return a_mem[x + 3], b_mem[x], d_mem[x]

    def prepare(i):
        rows_mem[i] = normed_rows(read, gain_column, columns[2 * i : 2 * i + 2])

    def post(i):
        xs = columns[2 * i : 2 * i + 2]
        store_tendency(raw.at[i], mask, xs, xs, t_mem)

    outs = []

    def send(low, high):
        for x in range(low, high):
            for f, new in enumerate((p_new, u_new, v_new)):
                new[x] = new[x] + t_mem[x, f]
        outs.extend(run_copies(
            [(new.at[low:high], out.at[low:high])
             for new, out in ((p_new, p_out), (u_new, u_out), (v_new, v_out))],
            sems, len(outs),
        ))

    def both(*works):
        def run():
            for work in works:
                work()
        return run

    def group(g):
        return lambda: dynamics(g)

    prepare(0)
    for copy in weights:
        copy.wait()
    w3[...] = w3t[...].T
    beside = (
        [group(0), group(1), group(2), lambda: prepare(1)],
        [group(3), group(4), group(5), both(lambda: prepare(2), lambda: post(0))],
        [group(6), group(7), both(lambda: post(1), lambda: send(0, 4)), lambda: send(4, 10)],
    )
    for i in range(3):
        network(rows_mem.at[i], w1, b1, w2, b2, w3, h1, h2, raw.at[i], beside[i])
    post(2)
    send(10, 12)
    for copy in outs:
        copy.wait()


def finish(p, u, v, left, right, tend, mid, weights, mask, courant, gain):
    shape = jax.ShapeDtypeStruct((WIDTH, LEVELS, ACROSS), F32)
    column = pltpu.VMEM((WIDTH, LEVELS, ACROSS), F32)
    return pl.pallas_call(
        finish_kernel,
        out_shape=(shape,) * 3,
        in_specs=[VMEM] * 5 + [ANY] * 7 + [VMEM] * 3,
        out_specs=(ANY,) * 3,
        scratch_shapes=[column] * 2
        + [pltpu.VMEM((WIDTH + 6, LEVELS, ACROSS), F32), column, column]
        + [pltpu.VMEM((7, LEVELS, ACROSS), F32)]
        + [pltpu.VMEM((WIDTH, 3, LEVELS, ACROSS), F32), pltpu.VMEM((3, LEVELS, 128), F32)]
        + [column] * 3
        + WEIGHTS_SCRATCH
        + [pltpu.SemaphoreType.DMA((17,))],
        compiler_params=pltpu.CompilerParams(vmem_limit_bytes=48 * 2**20),
        cost_estimate=pl.CostEstimate(
            flops=network_flops(WIDTH // 2 * ACROSS), bytes_accessed=12 * 2**20, transcendentals=0
        ),
        name="finish",
    )(p, u, v, left, right, tend, mid, *weights, mask, courant, gain)


def body(
    pressure, wind_x, wind_y, courant, send_list,
    norm_gain, w_first, b_first, w_second, b_second, w_last,
):
    p, u, v = [jnp.transpose(f, (1, 0, 2)) for f in (pressure, wind_x, wind_y)]
    courant, gain = courant.reshape(1, LEVELS), norm_gain.reshape(1, ROWS)
    lists = jnp.transpose(send_list, (2, 0, 1))
    weights = (w_first, b_first.reshape(1, UNITS), w_second, b_second.reshape(1, UNITS), w_last.T)
    to_next, to_prev = edges(p, u, v)
    left = lax.ppermute(to_next, AXES, [(i, (i + 1) % DEVICES) for i in range(DEVICES)])
    right = lax.ppermute(to_prev, AXES, [(i, (i - 1) % DEVICES) for i in range(DEVICES)])
    tend, mid, mask = interior(p, u, v, weights, courant, gain, lists)
    outs = finish(p, u, v, left, right, tend, mid, weights, mask, courant, gain)
    return tuple(jnp.transpose(f, (1, 0, 2)) for f in outs)


def solution(mesh):
    split = P(None, AXES, None)
    in_specs = (split,) * 3 + (P(), P(AXES, None, None)) + (P(),) * 6
    return jax.shard_map(
        body, mesh=mesh, in_specs=in_specs, out_specs=(split,) * 3, check_vma=False
    )
```

```python
import jax
import jax.numpy as jnp
from jax import lax
from jax.experimental import pallas as pl
from jax.experimental.pallas import tpu as pltpu
from jax.sharding import PartitionSpec as P

AXES = ("group", "tile")
LEVELS, WIDTH, ACROSS, UNITS, SLOTS, DEVICES = 60, 12, 384, 1024, 36, 128
ROWS = 3 * LEVELS
HALO = 6
SENT = 3 * HALO
CHUNK = 2 * ACROSS
TILE = 256
F32, BF16 = jnp.float32, jnp.bfloat16
NN = (((1,), (0,)), ((), ()))
NT = (((1,), (1,)), ((), ()))
ANY = pl.BlockSpec(memory_space=pltpu.HBM)
VMEM = pl.BlockSpec(memory_space=pltpu.VMEM)


def lanes(shape):
    return lax.broadcasted_iota(jnp.int32, shape, len(shape) - 1)


def split(value):
    return [value[:, i : i + 128] for i in range(0, ACROSS, 128)]


def join(parts):
    return jnp.concatenate(parts, axis=1)


def run_copies(pairs, sems, first=0):
    copies = [
        pltpu.make_async_copy(src, dst, sems.at[first + i]) for i, (src, dst) in enumerate(pairs)
    ]
    for copy in copies:
        copy.start()
    return copies


def divergence(v):
    v = jnp.where(lanes(v.shape) < ACROSS - 1, v, 0.0)
    return v - pltpu.roll(v, 1, 1)


def rest(value):
    return (value - value.astype(BF16).astype(F32)).astype(BF16)


def edges_kernel(p_hbm, u_hbm, v_hbm, r_mem, l_mem, p_mem, u_mem, v_mem, sems):
    low, high = slice(0, HALO), slice(WIDTH - HALO, WIDTH)
    loads = run_copies(
        [(f.at[s], m.at[s]) for s in (high, low)
         for f, m in ((p_hbm, p_mem), (u_hbm, u_mem), (v_hbm, v_mem))],
        sems,
    )
    loads[0].wait()
    for i in range(HALO):
        r_mem[i] = p_mem[WIDTH - HALO + i].astype(BF16)
    for i in range(3):
        r_mem[2 * HALO + i] = rest(p_mem[WIDTH - 1 - i])
    for copy in loads[1:3]:
        copy.wait()
    for i in range(HALO - 1):
        x = WIDTH - HALO + 1 + i
        div = (u_mem[x] - u_mem[x - 1]) + divergence(v_mem[x])
        r_mem[HALO + i] = div.astype(BF16)
        if x >= WIDTH - 2:
            r_mem[2 * HALO + 2 + WIDTH - x] = rest(div)
    r_mem[2 * HALO - 1] = u_mem[WIDTH - 1].astype(BF16)
    r_mem[SENT - 1] = rest(u_mem[WIDTH - 1])
    for copy in loads[3:]:
        copy.wait()
    for i in range(HALO):
        l_mem[i] = p_mem[i].astype(BF16)
    for x in range(HALO):
        west = u_mem[x - 1] if x else 0.0
        div = (u_mem[x] - west) + divergence(v_mem[x])
        l_mem[HALO + x] = div.astype(BF16)
        if x < 3:
            l_mem[2 * HALO + 3 + x] = rest(div)
    for i in range(3):
        l_mem[2 * HALO + i] = rest(p_mem[i])


def edges(p, u, v):
    shape = jax.ShapeDtypeStruct((SENT, LEVELS, ACROSS), BF16)
    return pl.pallas_call(
        edges_kernel,
        out_shape=(shape, shape),
        in_specs=[ANY] * 3,
        out_specs=(VMEM, VMEM),
        scratch_shapes=[pltpu.VMEM((WIDTH, LEVELS, ACROSS), F32)] * 3
        + [pltpu.SemaphoreType.DMA((6,))],
        compiler_params=pltpu.CompilerParams(vmem_limit_bytes=60 * 2**20),
        name="edges",
    )(p, u, v)


def stepping(count, low, high, square, load_p, load_d, done):
    ps = [{} for _ in range(count + 1)]
    ds = [{} for _ in range(count + 1)]
    sums = {}
    lane = lanes(square.shape)
    first, last = lane == 0, lane == 127

    def substep(k, x):
        west, here, east = (ps[k - 1][x + i] for i in (-1, 0, 1))
        down = [pltpu.roll(h, 127, 1) for h in here]
        up = [pltpu.roll(h, 1, 1) for h in here]
        north = [jnp.where(last, down[1], down[0]), jnp.where(last, down[2], down[1]),
                 jnp.where(last, here[2], down[2])]
        south = [jnp.where(first, here[0], up[0]), jnp.where(first, up[0], up[1]),
                 jnp.where(first, up[1], up[2])]
        ds[k][x] = [d - (((e + w) + (n + s)) - 4.0 * h)
                    for d, e, w, n, s, h in zip(ds[k - 1][x], east, west, north, south, here)]
        ps[k][x] = [h - square * d for h, d in zip(here, ds[k][x])]
        if k == count:
            done(x, ps[k][x], ds[k][x], sums[x], sums[x + 1])
        elif low + count - 1 <= x <= high - count + 1:
            sums[x] = [s + p for s, p in zip(sums[x], ps[k][x])]

    for t in range(low, high + 2 * count + 1):
        if t <= high:
            ps[0][t] = load_p(t)
            if low + count - 1 <= t <= high - count + 1:
                sums[t] = ps[0][t]
            if low < t < high:
                ds[0][t] = load_d(t)
        for k in range(1, count + 1):
            x = t - 2 * k
            if low + k <= x <= high - k:
                substep(k, x)
        yield


def march(*args):
    for _ in stepping(*args):
        pass


def march_both(one, two):
    for _ in zip(stepping(*one), stepping(*two), strict=True):
        pass


def own_divergence(u, west, v, inverse):
    lane = lanes(inverse.shape)
    first, last = lane == 0, lane == 127
    v = [v[0], v[1], jnp.where(last, 0.0, v[2])]
    up = [pltpu.roll(a, 1, 1) for a in v]
    south = [jnp.where(first, up[i - 1], up[i]) for i in range(3)]
    return [((a - w) + (b - s)) * inverse for a, w, b, s in zip(u, west, v, south)]


def winds(u, v, c, here, east):
    last = lanes(c.shape) == 127
    down = [pltpu.roll(s, 127, 1) for s in here]
    north = [jnp.where(last, down[1], down[0]), jnp.where(last, down[2], down[1]), down[2]]
    u = [a - c * (e - s) for a, e, s in zip(u, east, here)]
    v = [a - c * (n - s) for a, n, s in zip(v, north, here)]
    return u, [v[0], v[1], jnp.where(last, 0.0, v[2])]


def by_level(row):
    return jnp.broadcast_to(row, (128, row.shape[1])).T


def level_constants(courant_row, c_mem):
    c = by_level(courant_row)
    c_mem[0] = c
    c_mem[1] = c * c
    c_mem[2] = 1.0 / c


def group_rows(g):
    return pl.ds(8 * g, 8) if g < LEVELS // 8 else slice(LEVELS // 8 * 8, LEVELS)


def by_groups(work):
    def group(g, carry):
        work(pl.ds(pl.multiple_of(g * 8, 8), 8))
        return carry

    lax.fori_loop(0, LEVELS // 8, group, 0)
    work(group_rows(LEVELS // 8))


def silu(z):
    half = z * 0.5
    return half + half * jnp.tanh(half)


def normed_rows(read, gain, xs):
    columns = jnp.concatenate([jnp.concatenate(read(x), axis=0) for x in xs], axis=1)
    values = columns.astype(BF16).astype(F32)
    mean = jnp.sum(values * values, axis=0, keepdims=True) * (1.0 / ROWS)
    return (values * lax.rsqrt(mean + 1e-05) * gain).astype(BF16).T


def network(rows, w1, b1, w2, b2, w3, h1, h2, raw, beside=()):
    for n in range(0, UNITS, TILE):
        z = lax.dot_general(rows[...], w1[:, n : n + TILE], NN, preferred_element_type=F32)
        h1[:, n : n + TILE] = silu(z + b1[:, n : n + TILE]).astype(BF16)
    for n in range(0, UNITS, TILE):
        z = lax.dot_general(h1[...], w2[:, n : n + TILE], NN, preferred_element_type=F32)
        h2[:, n : n + TILE] = silu(z + b2[:, n : n + TILE]).astype(BF16)
        if n // TILE < len(beside):
            beside[n // TILE]()
    raw[...] = lax.dot_general(h2[...], w3[...], NN, preferred_element_type=F32)


def store_tendency(raw, mask, xs, places, out):
    t = raw[...].T.astype(BF16).astype(F32)
    for i, (x, place) in enumerate(zip(xs, places)):
        row = jnp.concatenate([mask[3 * x + j : 3 * x + j + 1, :] for j in range(3)], axis=1)
        listed = jnp.where(row > 0.5, t[:, i * ACROSS : (i + 1) * ACROSS], 0.0)
        for f in range(3):
            out[place, f] = listed[f * LEVELS : (f + 1) * LEVELS]


WEIGHTS_SCRATCH = [
    pltpu.VMEM((ROWS, UNITS), BF16),
    pltpu.VMEM((1, UNITS), F32),
    pltpu.VMEM((UNITS, UNITS), BF16),
    pltpu.VMEM((1, UNITS), F32),
    pltpu.VMEM((ROWS, UNITS), BF16),
    pltpu.VMEM((UNITS, ROWS), BF16),
    pltpu.VMEM((CHUNK, UNITS), BF16),
    pltpu.VMEM((CHUNK, UNITS), BF16),
    pltpu.VMEM((3, CHUNK, ROWS), BF16),
    pltpu.VMEM((3, CHUNK, ROWS), F32),
]


def network_flops(columns):
    return 2 * columns * (2 * ROWS * UNITS + UNITS * UNITS)


def interior_kernel(
    p_hbm, u_hbm, v_hbm, w1_hbm, b1_hbm, w2_hbm, b2_hbm, w3_hbm, courant, gain, lists,
    tend, mid, mask,
    p_mem, u_mem, v_mem, m_mem, t_mem, c_mem, one_x, one_y,
    w1, b1, w2, b2, w3t, w3, h1, h2, rows_mem, raw, sems,
):
    near, far = slice(0, 8), slice(8, WIDTH)
    fields = run_copies(
        [(f.at[s], m.at[s]) for s in (near, far)
         for f, m in ((p_hbm, p_mem), (u_hbm, u_mem), (v_hbm, v_mem))],
        sems,
    )
    weights = run_copies([(w3_hbm, w3t), (w1_hbm, w1), (b1_hbm, b1), (w2_hbm, w2), (b2_hbm, b2)],
                         sems, 6)
    level_constants(courant[...], c_mem)
    gain_column = by_level(gain[...])[:, :1]
    for s in range(SLOTS):
        entry = lists[s]
        part, spot = entry >> 7, entry & 127
        where = slice(s * DEVICES, (s + 1) * DEVICES)
        one_x[:, where] = (
            lax.broadcasted_iota(jnp.int32, (48, DEVICES), 0) == part
        ).astype(F32).astype(BF16)
        one_y[:, where] = (
            lax.broadcasted_iota(jnp.int32, (128, DEVICES), 0) == spot
        ).astype(F32).astype(BF16)
    mask[...] = lax.dot_general(one_x[...], one_y[...], NT, preferred_element_type=F32)

    def columns(rows, *pairs):
        c, square, inverse = (c_mem[j, rows, :] for j in range(3))

        def done(x, p, d, here, east):
            u, v = winds(split(u_mem[x, rows, :]), split(v_mem[x, rows, :]), c, here, east)
            for f, value in enumerate((p, u, v)):
                m_mem[f, x - 3, rows, :] = join(value)

        def load_d(x):
            return own_divergence(split(u_mem[x, rows, :]), split(u_mem[x - 1, rows, :]),
                                  split(v_mem[x, rows, :]), inverse)

        return [(3, 2 * i, 2 * i + 7, square, lambda x: split(p_mem[x, rows, :]), load_d, done)
                for i in pairs]

    def first_pair(rows, more):
        march_both(*columns(rows, 0), *columns(more, 0))

    def two_groups(g, carry):
        at = pl.multiple_of(g * 16, 16)
        first_pair(pl.ds(at, 8), pl.ds(pl.multiple_of(at + 8, 8), 8))
        return carry

    def other_pairs(low, high):
        def run():
            for g in range(low, high):
                march_both(*columns(group_rows(g), 1, 2))
        return run

    def read(x):
        return [m_mem[f, x] for f in range(3)]

    def prepare(i):
        rows_mem[i] = normed_rows(read, gain_column, (2 * i, 2 * i + 1))

    sent = []

    def post(i):
        xs = (2 * i, 2 * i + 1)
        store_tendency(raw.at[i], mask, [x + 3 for x in xs], xs, t_mem)
        sent.extend(run_copies([(t_mem.at[2 * i : 2 * i + 2], tend.at[2 * i : 2 * i + 2])],
                               sems, 11 + i))

    def both(*works):
        def run():
            for work in works:
                work()
        return run

    for copy in fields[:3]:
        copy.wait()
    lax.fori_loop(0, LEVELS // 16, two_groups, 0)
    first_pair(group_rows(6), group_rows(7))
    for copy in fields[3:]:
        copy.wait()
    prepare(0)
    for copy in weights:
        copy.wait()
    w3[...] = w3t[...].T
    beside = (
        [other_pairs(0, 2), other_pairs(2, 4), other_pairs(4, 6),
         both(other_pairs(6, 8), lambda: prepare(1))],
        [lambda: post(0), lambda: prepare(2)],
        [lambda: sent.extend(run_copies([(m_mem, mid)], sems, 14)), lambda: post(1)],
    )
    for i in range(3):
        network(rows_mem.at[i], w1, b1, w2, b2, w3, h1, h2, raw.at[i], beside[i])
    post(2)
    for copy in sent:
        copy.wait()


def interior(p, u, v, weights, courant, gain, lists):
    column = pltpu.VMEM((WIDTH, LEVELS, ACROSS), F32)
    return pl.pallas_call(
        interior_kernel,
        out_shape=(
            jax.ShapeDtypeStruct((WIDTH // 2, 3, LEVELS, ACROSS), F32),
            jax.ShapeDtypeStruct((3, WIDTH // 2, LEVELS, ACROSS), F32),
            jax.ShapeDtypeStruct((48, 128), F32),
        ),
        in_specs=[ANY] * 8 + [VMEM] * 3,
        out_specs=(ANY, ANY, VMEM),
        scratch_shapes=[column] * 3
        + [pltpu.VMEM((3, WIDTH // 2, LEVELS, ACROSS), F32)]
        + [pltpu.VMEM((WIDTH // 2, 3, LEVELS, ACROSS), F32), pltpu.VMEM((3, LEVELS, 128), F32)]
        + [pltpu.VMEM((48, SLOTS * DEVICES), BF16), pltpu.VMEM((128, SLOTS * DEVICES), BF16)]
        + WEIGHTS_SCRATCH
        + [pltpu.SemaphoreType.DMA((15,))],
        compiler_params=pltpu.CompilerParams(vmem_limit_bytes=52 * 2**20),
        cost_estimate=pl.CostEstimate(
            flops=network_flops(WIDTH // 2 * ACROSS), bytes_accessed=8 * 2**20, transcendentals=0
        ),
        name="interior",
    )(p, u, v, *weights, courant, gain, lists)


def finish_kernel(
    p_own, u_mem, v_mem, left, right, tend, mid, w1_hbm, b1_hbm, w2_hbm, b2_hbm, w3_hbm,
    mask, courant, gain,
    p_out, u_out, v_out,
    p_mem, e_mem, a_mem, b_mem, d_mem, g_mem, t_mem, c_mem,
    p_new, u_new, v_new,
    w1, b1, w2, b2, w3t, w3, h1, h2, rows_mem, raw, sems,
):
    weights = run_copies(
        [(w3_hbm, w3t), (w1_hbm, w1), (b1_hbm, b1), (w2_hbm, w2), (b2_hbm, b2),
         (mid.at[0], a_mem.at[6:12]), (mid.at[1], b_mem.at[3:9]), (mid.at[2], d_mem.at[3:9]),
         (tend, t_mem.at[3:9])],
        sems, 8,
    )
    level_constants(courant[...], c_mem)
    gain_column = by_level(gain[...])[:, :1]

    def loads(rows, inverse):
        def load_p(x):
            if 0 <= x < WIDTH:
                return split(p_own[x, rows, :])
            return split(p_mem[x + HALO if x < 0 else x - HALO, rows, :])

        def load_d(x):
            if x < 0:
                return [d * inverse for d in split(e_mem[x + HALO - 1, rows, :])]
            if x > WIDTH:
                return [d * inverse for d in split(e_mem[x - HALO, rows, :])]
            if x == WIDTH:
                return [(d - u) * inverse for d, u in zip(split(e_mem[HALO, rows, :]),
                                                          split(u_mem[WIDTH - 1, rows, :]))]
            west = u_mem[x - 1, rows, :] if x else e_mem[HALO - 1, rows, :]
            return own_divergence(split(u_mem[x, rows, :]), split(west),
                                  split(v_mem[x, rows, :]), inverse)

        return load_p, load_d

    def strips(rows):
        c, square, inverse = (c_mem[i, rows, :] for i in range(3))

        def done(x, p, d, here, east):
            a_mem[x + 3, rows, :] = join(p)
            u, v = winds(split(u_mem[x, rows, :]), split(v_mem[x, rows, :]), c, here, east)
            b_mem[x, rows, :] = join(u)
            d_mem[x, rows, :] = join(v)
            if x == 0:
                g_mem[3, rows, :] = join(d)

        common = (square, *loads(rows, inverse), done)
        march_both((3, -3, 5, *common), (3, 6, 14, *common))

    for i in range(HALO):
        p_mem[i] = left[i].astype(F32)
        e_mem[i] = left[HALO + i].astype(F32)
        p_mem[HALO + i] = right[i].astype(F32)
        e_mem[HALO + i] = right[HALO + i].astype(F32)
    for i, (near_p, near_e) in enumerate(((1, 2), (2, 3), (3, 1))):
        p_mem[HALO - near_p] = p_mem[HALO - near_p] + left[2 * HALO + i].astype(F32)
        e_mem[HALO - near_e] = e_mem[HALO - near_e] + left[2 * HALO + 3 + i].astype(F32)
        p_mem[HALO + i] = p_mem[HALO + i] + right[2 * HALO + i].astype(F32)
        e_mem[HALO + i] = e_mem[HALO + i] + right[2 * HALO + 3 + i].astype(F32)
    by_groups(strips)

    def dynamics(g):
        rows = group_rows(g)
        c, square, inverse = (c_mem[i, rows, :] for i in range(3))

        def outer(x, p, d, here, east):
            a_mem[x + 3, rows, :] = join(p)
            g_mem[x + 3 if x < 0 else x - 8, rows, :] = join(d)

        common = (square, *loads(rows, inverse), outer)
        march_both((3, -6, 2, *common), (3, 9, 17, *common))

        def load_d(x):
            if 0 < x < WIDTH:
                return own_divergence(split(b_mem[x, rows, :]), split(b_mem[x - 1, rows, :]),
                                      split(d_mem[x, rows, :]), inverse)
            return split(g_mem[x + 3 if x <= 0 else x - 8, rows, :])

        def done(x, p, d, here, east):
            p_new[x, rows, :] = join(p)
            u, v = winds(split(b_mem[x, rows, :]), split(d_mem[x, rows, :]), c, here, east)
            u_new[x, rows, :] = join(u)
            v_new[x, rows, :] = join(v)

        march(3, -3, 14, square, lambda x: split(a_mem[x + 3, rows, :]), load_d, done)

    columns = (0, 1, 2, 9, 10, 11)

    def read(x):
        return a_mem[x + 3], b_mem[x], d_mem[x]

    def prepare(i):
        rows_mem[i] = normed_rows(read, gain_column, columns[2 * i : 2 * i + 2])

    def post(i):
        xs = columns[2 * i : 2 * i + 2]
        store_tendency(raw.at[i], mask, xs, xs, t_mem)

    outs = []

    def send(low, high):
        for x in range(low, high):
            for f, new in enumerate((p_new, u_new, v_new)):
                new[x] = new[x] + t_mem[x, f]
        outs.extend(run_copies(
            [(new.at[low:high], out.at[low:high])
             for new, out in ((p_new, p_out), (u_new, u_out), (v_new, v_out))],
            sems, len(outs),
        ))

    def both(*works):
        def run():
            for work in works:
                work()
        return run

    def group(g):
        return lambda: dynamics(g)

    prepare(0)
    for copy in weights:
        copy.wait()
    w3[...] = w3t[...].T
    beside = (
        [group(0), group(1), group(2), lambda: prepare(1)],
        [group(3), group(4), group(5), both(lambda: prepare(2), lambda: post(0))],
        [group(6), group(7), both(lambda: post(1), lambda: send(0, 4)), lambda: send(4, 10)],
    )
    for i in range(3):
        network(rows_mem.at[i], w1, b1, w2, b2, w3, h1, h2, raw.at[i], beside[i])
    post(2)
    send(10, 12)
    for copy in outs:
        copy.wait()


def finish(p, u, v, left, right, tend, mid, weights, mask, courant, gain):
    shape = jax.ShapeDtypeStruct((WIDTH, LEVELS, ACROSS), F32)
    column = pltpu.VMEM((WIDTH, LEVELS, ACROSS), F32)
    return pl.pallas_call(
        finish_kernel,
        out_shape=(shape,) * 3,
        in_specs=[VMEM] * 5 + [ANY] * 7 + [VMEM] * 3,
        out_specs=(ANY,) * 3,
        scratch_shapes=[column] * 2
        + [pltpu.VMEM((WIDTH + 6, LEVELS, ACROSS), F32), column, column]
        + [pltpu.VMEM((7, LEVELS, ACROSS), F32)]
        + [pltpu.VMEM((WIDTH, 3, LEVELS, ACROSS), F32), pltpu.VMEM((3, LEVELS, 128), F32)]
        + [column] * 3
        + WEIGHTS_SCRATCH
        + [pltpu.SemaphoreType.DMA((17,))],
        compiler_params=pltpu.CompilerParams(vmem_limit_bytes=48 * 2**20),
        cost_estimate=pl.CostEstimate(
            flops=network_flops(WIDTH // 2 * ACROSS), bytes_accessed=12 * 2**20, transcendentals=0
        ),
        name="finish",
    )(p, u, v, left, right, tend, mid, *weights, mask, courant, gain)


def body(
    pressure, wind_x, wind_y, courant, send_list,
    norm_gain, w_first, b_first, w_second, b_second, w_last,
):
    p, u, v = [jnp.transpose(f, (1, 0, 2)) for f in (pressure, wind_x, wind_y)]
    courant, gain = courant.reshape(1, LEVELS), norm_gain.reshape(1, ROWS)
    lists = jnp.transpose(send_list, (2, 0, 1))
    weights = (w_first, b_first.reshape(1, UNITS), w_second, b_second.reshape(1, UNITS), w_last.T)
    to_next, to_prev = edges(p, u, v)
    left = lax.ppermute(to_next, AXES, [(i, (i + 1) % DEVICES) for i in range(DEVICES)])
    right = lax.ppermute(to_prev, AXES, [(i, (i - 1) % DEVICES) for i in range(DEVICES)])
    tend, mid, mask = interior(p, u, v, weights, courant, gain, lists)
    outs = finish(p, u, v, left, right, tend, mid, weights, mask, courant, gain)
    return tuple(jnp.transpose(f, (1, 0, 2)) for f in outs)


def solution(mesh):
    split = P(None, AXES, None)
    in_specs = (split,) * 3 + (P(), P(AXES, None, None)) + (P(),) * 6
    return jax.shard_map(
        body, mesh=mesh, in_specs=in_specs, out_specs=(split,) * 3, check_vma=False
    )
```
